32 devices in a mesh: inp: 4 (over z), wt: 4 (over x, core), dep: 2 (over y).
Axes of the slice: x: 2, y: 2, z: 4, core: 2. Of those that a mesh axis runs over, the one named last changes fastest.
Arguments:
- x_saved: bfloat16 [1024, 8192], P(('wt', 'dep'), 'inp'), may hold values from -6 to 6
- out_grad: bfloat16 [1024, 8192], P(('wt', 'dep'), 'inp'), may hold values from -6 to 6
- gate_pre: bfloat16 [1024, 29568], P('inp', ('wt', 'dep')), may hold values from -6 to 6
- up_pre: bfloat16 [1024, 29568], P('inp', ('wt', 'dep')), may hold values from -6 to 6
- w_gate: bfloat16 [8192, 29568], P('inp', ('wt', 'dep')), may hold values from -0.0625 to 0.0625
- w_up: bfloat16 [8192, 29568], P('inp', ('wt', 'dep')), may hold values from -0.0625 to 0.0625
- w_down: bfloat16 [29568, 8192], P(('wt', 'dep'), 'inp'), may hold values from -0.03125 to 0.03125
Outputs:
- input_grad: bfloat16 [1024, 8192], P(('wt', 'dep'), 'inp')
- gate_wgrad: bfloat16 [8192, 29568], P('inp', ('wt', 'dep'))
- up_wgrad: bfloat16 [8192, 29568], P('inp', ('wt', 'dep'))
- down_wgrad: bfloat16 [29568, 8192], P(('wt', 'dep'), 'inp')
The draws below stay inside these ranges and needn't reach their ends.
All inputs are finite; a program needn't handle non-finite values.
Results may differ from the reference program's by a relative error of at most 0.005.
Values may be sent and summed in bfloat16 or wider, within the bound.
No kernel may reach another device: no remote copies, remote signals or barrier semaphores. Data moves between devices by JAX's collectives and lax.ppermute only.
A program may use at most 192 MiB of HBM per device.

```python
import jax
import jax.numpy as jnp
from jax import lax

D = 8192
FF = 29568
TOKENS = 1024


def block_levels(key, dims, shards, least, largest):
    def one(position, blocks):
        draws = jax.random.uniform(jax.random.fold_in(jax.random.fold_in(key, 6), position), (blocks,), jnp.float32, least / len(shards), largest / len(shards))
        return jnp.repeat(jnp.exp(draws), dims[position] // blocks).reshape((-1,) + (1,) * (len(dims) - position - 1))

    gain = one(*shards[0])
    for cut in shards[1:]:
        gain = gain * one(*cut)
    return gain


def gaussian(key, extent, deviation, reach, cuts=(), held_as=jnp.bfloat16):
    factor_of = block_levels(key, extent, cuts, -0.22, 0.18) if cuts else 1.0
    values = jax.random.normal(key, extent, jnp.float32) * deviation * factor_of
    return jnp.minimum(jnp.maximum(values, -reach), reach).astype(held_as)


def setup_inputs(seed: int = 0) -> dict:
    keys = jax.random.split(jax.random.key(seed), 8)
    x_saved = gaussian(keys[0], (TOKENS, D), 1.0, 6.0, ((0, 8), (1, 4)))
    out_grad = gaussian(keys[1], (TOKENS, D), 1.0, 6.0, ((0, 8), (1, 4)))
    gate_pre = gaussian(keys[2], (TOKENS, FF), 1.5, 6.0, ((0, 4), (1, 8)))
    up_pre = gaussian(keys[3], (TOKENS, FF), 1.0, 6.0, ((0, 4), (1, 8)))
    w_gate = gaussian(keys[4], (D, FF), D ** -0.5, 0.0625, ((0, 4), (1, 8)))
    w_up = gaussian(keys[5], (D, FF), D ** -0.5, 0.0625, ((0, 4), (1, 8)))
    w_down = gaussian(keys[6], (FF, D), FF ** -0.5, 0.03125, ((0, 8), (1, 4)))
    return {"x_saved": x_saved, "out_grad": out_grad, "gate_pre": gate_pre, "up_pre": up_pre, "w_gate": w_gate, "w_up": w_up, "w_down": w_down}


def reference(x_saved, out_grad, gate_pre, up_pre, w_gate, w_up, w_down):
    hidden_grad = lax.dot_general(out_grad, w_down, (((1,), (1,)), ((), ())), preferred_element_type=jnp.float32)
    gate = gate_pre.astype(jnp.float32)
    upper = up_pre.astype(jnp.float32)
    sigma = jax.nn.sigmoid(gate)
    active = gate * sigma
    hidden = (active * upper).astype(jnp.bfloat16)
    up_act_grad = (hidden_grad * active).astype(jnp.bfloat16)
    gate_act_grad = (hidden_grad * upper * sigma * (1.0 + gate * (1.0 - sigma))).astype(jnp.bfloat16)
    down_wgrad = lax.dot_general(hidden, out_grad, (((0,), (0,)), ((), ())), preferred_element_type=jnp.float32).astype(jnp.bfloat16)
    gate_wgrad = lax.dot_general(x_saved, gate_act_grad, (((0,), (0,)), ((), ())), preferred_element_type=jnp.float32).astype(jnp.bfloat16)
    up_wgrad = lax.dot_general(x_saved, up_act_grad, (((0,), (0,)), ((), ())), preferred_element_type=jnp.float32).astype(jnp.bfloat16)
    input_grad = lax.dot_general(gate_act_grad, w_gate, (((1,), (1,)), ((), ())), preferred_element_type=jnp.float32)
    input_grad = input_grad + lax.dot_general(up_act_grad, w_up, (((1,), (1,)), ((), ())), preferred_element_type=jnp.float32)
    return input_grad.astype(jnp.bfloat16), gate_wgrad, up_wgrad, down_wgrad
```

```python
import functools

import jax
import jax.numpy as jnp
from jax import lax
from jax.experimental import pallas as pl
from jax.experimental.pallas import tpu as pltpu
from jax.sharding import PartitionSpec as P

GROUPS = 4
VMEM_LIMIT = 60 * 1024 * 1024

SWAP = [(0, 1), (1, 0), (2, 3), (3, 2)]
MIDDLE = [(1, 2), (2, 1)]
TO_ENDS = [(1, 0), (2, 3)]


def send(value, pairs):
    return lax.ppermute(value, "inp", pairs)


def block_rows(rows):
    units = rows // 16
    return 16 * max(n for n in range(1, 33) if units % n == 0)


def sum_kernel(w_ref, grad_ref, out_ref):
    count, _, width = out_ref.shape
    for j in range(count):
        out_ref[j] = lax.dot_general(
            w_ref[...],
            grad_ref[j * width : (j + 1) * width, :],
            (((1,), (1,)), ((), ())),
            preferred_element_type=jnp.float32,
        )


def slot_value(end, refs, slot):
    if slot == 0:
        return refs[0][...].astype(jnp.float32)
    if slot == 1:
        return refs[1][...].astype(jnp.float32)
    at_end, at_middle = refs[2:4] if slot == 2 else refs[4:6]
    return jnp.where(end, at_end[...], at_middle[...]).astype(jnp.float32)


def place(k_ref, slot):
    return k_ref[0] ^ slot


def columns(index, width):
    return pl.ds(pl.multiple_of(index * width, width), width)


def valid_rows(value, rows, block):
    at = lax.broadcasted_iota(jnp.int32, value.shape, 0) + pl.program_id(0) * block
    return jnp.where(at < rows, value, jnp.zeros_like(value))


def down_kernel(k_ref, *refs):
    gates, uppers = refs[:6], refs[6:12]
    grad_ref, out_ref, hidden = refs[12], refs[-2], refs[-1]
    width = gates[0].shape[1]
    end = k_ref[1] == 1
    for slot in range(4):
        gate, upper = slot_value(end, gates, slot), slot_value(end, uppers, slot)
        value = gate * jax.nn.sigmoid(gate) * upper
        hidden[:, columns(place(k_ref, slot), width)] = value.astype(jnp.bfloat16)
    features = grad_ref.shape[1]
    step = min(features, 512)
    for c in range(0, features, step):
        cols = slice(c, c + step)
        out_ref[:, cols] = jnp.dot(
            hidden[...], grad_ref[:, cols], preferred_element_type=jnp.float32
        ).astype(jnp.bfloat16)


def main_kernel(rows, has_acc, k_ref, *refs):
    gates, uppers = refs[:6], refs[6:12]
    part, r1, r2, r3, x_ref, wg_ref, wu_ref = refs[12:19]
    acc_in = refs[19] if has_acc else None
    acc, gate_out, up_out, gate_grad, up_grad = refs[-5:]
    block, width = gates[0].shape
    ragged = rows % block != 0
    end = k_ref[1] == 1
    for slot in range(4):
        gate, upper = slot_value(end, gates, slot), slot_value(end, uppers, slot)
        j = place(k_ref, slot)
        at = columns(j, width)
        hidden_grad = (
            part[j]
            + r2[j].astype(jnp.float32)
            + jnp.where(end, r3[j], r1[j]).astype(jnp.float32)
        )
        sigma = jax.nn.sigmoid(gate)
        up_value = (hidden_grad * (gate * sigma)).astype(jnp.bfloat16)
        gate_value = (
            hidden_grad * upper * sigma * (1.0 + gate * (1.0 - sigma))
        ).astype(jnp.bfloat16)
        if ragged:
            up_value = valid_rows(up_value, rows, block)
            gate_value = valid_rows(gate_value, rows, block)
        up_grad[:, at] = up_value
        gate_grad[:, at] = gate_value

    @pl.when(pl.program_id(0) == 0)
    def _():
        if has_acc:
            acc[...] = acc_in[...]
        else:
            acc[...] = jnp.zeros_like(acc)

    features = x_ref.shape[1]
    step = min(features, 512)
    for c in range(0, features, step):
        cols = slice(c, c + step)
        gate_out[:, cols] = jnp.dot(
            gate_grad[...], x_ref[:, cols], preferred_element_type=jnp.float32
        ).astype(jnp.bfloat16)
        up_out[:, cols] = jnp.dot(
            up_grad[...], x_ref[:, cols], preferred_element_type=jnp.float32
        ).astype(jnp.bfloat16)
        wg, wu = wg_ref[:, cols], wu_ref[:, cols]
        if ragged:
            wg, wu = valid_rows(wg, rows, block), valid_rows(wu, rows, block)
        dims = (((0,), (0,)), ((), ()))
        acc[:, cols] += lax.dot_general(
            gate_grad[...], wg, dims, preferred_element_type=jnp.float32
        ) + lax.dot_general(
            up_grad[...], wu, dims, preferred_element_type=jnp.float32
        )


def once(shape):
    return pl.BlockSpec(shape, lambda i, *k: (0, 0), pipeline_mode=pl.Buffered(1))


def sum_group(w_down, grad_whole, a, size, count):
    tokens, features = grad_whole.shape
    block = block_rows(size)
    blocks = size // block
    width = tokens // count
    return pl.pallas_call(
        sum_kernel,
        grid=(blocks,),
        in_specs=[
            pl.BlockSpec((block, features), lambda i: (a * blocks + i, 0)),
            once((tokens, features)),
        ],
        out_specs=pl.BlockSpec((count, block, width), lambda i: (0, i, 0)),
        out_shape=jax.ShapeDtypeStruct((count, size, width), jnp.float32),
        compiler_params=pltpu.CompilerParams(vmem_limit_bytes=VMEM_LIMIT),
        cost_estimate=pl.CostEstimate(
            flops=2 * size * tokens * features,
            bytes_accessed=size * (features * 2 + tokens * 4),
            transcendentals=0,
        ),
    )(w_down, grad_whole)


def slot_specs(a, block, width):
    gate = pl.BlockSpec((None, block, width), lambda i, k: (a % 2, i, 0))
    upper = pl.BlockSpec((None, block, width), lambda i, k: (2 + a % 2, i, 0))
    return [gate] * 6 + [upper] * 6


def down_group(k, slots, grad_whole, out, a, size, total):
    tokens, features = grad_whole.shape
    width = slots[0].shape[2]
    block = block_rows(size)
    blocks = size // block
    specs = slot_specs(a, block, width) + [once((tokens, features))]
    args = list(slots) * 2 + [grad_whole]
    aliases = {}
    if out is not None:
        aliases[1 + len(args)] = 0
        args.append(out)
        specs.append(pl.BlockSpec(memory_space=pl.ANY))
    return pl.pallas_call(
        down_kernel,
        grid_spec=pltpu.PrefetchScalarGridSpec(
            num_scalar_prefetch=1,
            grid=(blocks,),
            in_specs=specs,
            out_specs=pl.BlockSpec(
                (block, features), lambda i, k: (a * blocks + i, 0)
            ),
            scratch_shapes=[pltpu.VMEM((block, tokens), jnp.bfloat16)],
        ),
        out_shape=jax.ShapeDtypeStruct((total, features), jnp.bfloat16),
        input_output_aliases=aliases,
        compiler_params=pltpu.CompilerParams(vmem_limit_bytes=VMEM_LIMIT),
        cost_estimate=pl.CostEstimate(
            flops=2 * size * tokens * features,
            bytes_accessed=size * (features * 2 + tokens * 4),
            transcendentals=size * tokens,
        ),
    )(k, *args)


def main_group(k, slots, sums, x_whole, wg, wu, acc, outs, a, size, total):
    tokens, features = x_whole.shape
    count, _, width = slots[0].shape
    block = block_rows(size)
    blocks = size // block
    wide = pl.BlockSpec((count, block, width), lambda i, k: (0, i, 0))
    weight = pl.BlockSpec((block, features), lambda i, k: (a * blocks + i, 0))
    specs = (
        slot_specs(a, block, width)
        + [wide] * 4
        + [once((tokens, features)), weight, weight]
    )
    args = list(slots) * 2 + list(sums) + [x_whole, wg, wu]
    aliases = {}
    if acc is not None:
        aliases[1 + len(args)] = 0
        args.append(acc)
        specs.append(once((tokens, features)))
        for i, out in enumerate(outs):
            aliases[1 + len(args)] = 1 + i
            args.append(out)
            specs.append(pl.BlockSpec(memory_space=pl.ANY))
    wgrad = jax.ShapeDtypeStruct((total, features), jnp.bfloat16)
    rows = min(size, total - a * size)
    return pl.pallas_call(
        functools.partial(main_kernel, rows, acc is not None),
        grid_spec=pltpu.PrefetchScalarGridSpec(
            num_scalar_prefetch=1,
            grid=(blocks,),
            in_specs=specs,
            out_specs=(once((tokens, features)), weight, weight),
            scratch_shapes=[pltpu.VMEM((block, tokens), jnp.bfloat16)] * 2,
        ),
        out_shape=(
            jax.ShapeDtypeStruct((tokens, features), jnp.float32),
            wgrad,
            wgrad,
        ),
        input_output_aliases=aliases,
        compiler_params=pltpu.CompilerParams(vmem_limit_bytes=VMEM_LIMIT),
        cost_estimate=pl.CostEstimate(
            flops=8 * size * tokens * features,
            bytes_accessed=size * (features * 8 + tokens * 14),
            transcendentals=size * tokens,
        ),
    )(k, *args)


def scatter_axis(value, axis, name, size):
    me = lax.axis_index(name)
    bit = 1
    while bit < size:
        shape = value.shape
        high = size // (2 * bit)
        view = value.reshape(shape[:axis] + (high, 2) + shape[axis + 1 :])
        mine = (me // bit) % 2
        pairs = [(i, i ^ bit) for i in range(size)]
        away = lax.dynamic_index_in_dim(view, 1 - mine, axis + 1, keepdims=False)
        kept = lax.dynamic_index_in_dim(view, mine, axis + 1, keepdims=False)
        got = lax.ppermute(away.astype(jnp.bfloat16), name, pairs)
        value = kept.astype(jnp.float32) + got.astype(jnp.float32)
        bit *= 2
    return value.reshape(value.shape[:axis] + value.shape[axis + 1 :])


def own_half(gate, upper, half, size):
    first, last = 2 * half * size, 2 * (half + 1) * size
    parts = []
    for whole in (gate, upper):
        part = whole[first : min(last, whole.shape[0])]
        part = jnp.pad(part, ((0, last - first - part.shape[0]), (0, 0)))
        parts.append(part.reshape(2, size, -1))
    return jnp.concatenate(parts, axis=0)


def per_device(n_wt, n_dep, x_saved, out_grad, gate_pre, up_pre, w_gate, w_up, w_down):
    index = lax.axis_index("inp")
    end = (index == 0) | (index == 3)
    k = jnp.stack([index, end]).astype(jnp.int32)
    total = w_down.shape[0]
    size = 16 * -(-total // (16 * GROUPS))
    gate, upper = gate_pre.T, up_pre.T
    wg, wu = w_gate.T, w_up.T

    def rounded(part, got):
        return (part + got.astype(jnp.float32)).astype(jnp.bfloat16)

    own = [own_half(gate, upper, half, size) for half in range(2)]
    swap, middle = [], []
    for step in range(2):
        swap.append(send(own[step], SWAP))
        middle.append(send(own[step], MIDDLE))
    x_whole, grad_whole = (
        lax.all_gather(x_saved, ("wt", "dep"), axis=0, tiled=True),
        lax.all_gather(out_grad, ("wt", "dep"), axis=0, tiled=True),
    )
    part = [sum_group(w_down, grad_whole, a, size, 4) for a in range(GROUPS)]
    for step in range(2, 10):
        if step < 6:
            outward = part[step - 2].astype(jnp.bfloat16)
            payload = jnp.where(end, outward, middle[step - 2])
            swap.append(send(payload, SWAP))
        else:
            swap.append(send(rounded(part[step - 6], middle[step - 2]), TO_ENDS))
        if step < 4:
            middle.append(send(swap[step - 2], MIDDLE))
        elif step < 8:
            middle.append(send(rounded(part[step - 4], swap[step - 2]), MIDDLE))

    down = None
    acc, wgrads = None, (None, None)
    for a in range(GROUPS):
        h = a // 2
        slots = [own[h], swap[h], swap[2 + h], middle[2 + h], swap[4 + h], middle[h]]
        down = down_group(k, slots, grad_whole, down, a, size, total)
        sums = [part[a], swap[2 + a], middle[4 + a], swap[6 + a]]
        acc, *wgrads = main_group(
            k, slots, sums, x_whole, wg, wu, acc, wgrads, a, size, total
        )
    gate_wgrad, up_wgrad = wgrads

    tokens, features = acc.shape
    view = acc.reshape(n_wt, n_dep, tokens // (n_wt * n_dep), features)
    input_grad = scatter_axis(view, 0, "wt", n_wt)
    input_grad = scatter_axis(input_grad, 0, "dep", n_dep)
    return (input_grad.astype(jnp.bfloat16), gate_wgrad.T, up_wgrad.T, down)


def solution(mesh):
    placed = (
        P(("wt", "dep"), "inp"),
        P(("wt", "dep"), "inp"),
        P("inp", ("wt", "dep")),
        P("inp", ("wt", "dep")),
        P("inp", ("wt", "dep")),
        P("inp", ("wt", "dep")),
        P(("wt", "dep"), "inp"),
    )
    return jax.shard_map(
        functools.partial(per_device, mesh.shape["wt"], mesh.shape["dep"]),
        mesh=mesh,
        in_specs=placed,
        out_specs=(
            P(("wt", "dep"), "inp"),
            P("inp", ("wt", "dep")),
            P("inp", ("wt", "dep")),
            P(("wt", "dep"), "inp"),
        ),
        check_vma=False,
    )
```

```python
import functools

import jax
import jax.numpy as jnp
from jax import lax
from jax.experimental import pallas as pl
from jax.experimental.pallas import tpu as pltpu
from jax.sharding import PartitionSpec as P

GROUPS = 4
VMEM_LIMIT = 60 * 1024 * 1024

SWAP = [(0, 1), (1, 0), (2, 3), (3, 2)]
MIDDLE = [(1, 2), (2, 1)]
TO_ENDS = [(1, 0), (2, 3)]


def tie(value, *after):
    return pl.pallas_call(
        lambda *refs: None,
        in_specs=[pl.BlockSpec(memory_space=pl.ANY)] * (1 + len(after)),
        out_specs=pl.BlockSpec(memory_space=pl.ANY),
        out_shape=jax.ShapeDtypeStruct(value.shape, value.dtype),
        input_output_aliases={0: 0},
    )(value, *after)


def send(value, pairs):
    return lax.ppermute(value, "inp", pairs)


def block_rows(rows):
    units = rows // 16
    return 16 * max(n for n in range(1, 33) if units % n == 0)


def sum_kernel(w_ref, grad_ref, out_ref):
    count, _, width = out_ref.shape
    for j in range(count):
        out_ref[j] = lax.dot_general(
            w_ref[...],
            grad_ref[j * width : (j + 1) * width, :],
            (((1,), (1,)), ((), ())),
            preferred_element_type=jnp.float32,
        )


def sigmoid(value):
    return 0.5 + 0.5 * jnp.tanh(0.5 * value)


def slot_value(end, refs, slot):
    if slot == 0:
        return refs[0][...].astype(jnp.float32)
    if slot == 1:
        return refs[1][...].astype(jnp.float32)
    at_end, at_middle = refs[2:4] if slot == 2 else refs[4:6]
    return jnp.where(end, at_end[...], at_middle[...]).astype(jnp.float32)


def place(k_ref, slot):
    return k_ref[0] ^ slot


def columns(index, width):
    return pl.ds(pl.multiple_of(index * width, width), width)


def valid_rows(value, rows, block):
    at = lax.broadcasted_iota(jnp.int32, value.shape, 0) + pl.program_id(0) * block
    return jnp.where(at < rows, value, jnp.zeros_like(value))


def down_kernel(factors, k_ref, *refs):
    gates, uppers = refs[:6], refs[6:12]
    grad_ref, hidden = refs[12], refs[-1]
    out_ref = refs[-4] if factors else refs[-2]
    width = gates[0].shape[1]
    end = k_ref[1] == 1
    for slot in range(4):
        gate, upper = slot_value(end, gates, slot), slot_value(end, uppers, slot)
        j = place(k_ref, slot)
        sigma = sigmoid(gate)
        active = gate * sigma
        hidden[:, columns(j, width)] = (active * upper).astype(jnp.bfloat16)
        if factors:
            refs[-3][j] = active
            refs[-2][j] = upper * sigma * (1.0 + gate * (1.0 - sigma))
    features = grad_ref.shape[1]
    step = min(features, 512)
    for c in range(0, features, step):
        cols = slice(c, c + step)
        out_ref[:, cols] = jnp.dot(
            hidden[...], grad_ref[:, cols], preferred_element_type=jnp.float32
        ).astype(jnp.bfloat16)


def main_kernel(rows, has_acc, k_ref, *refs):
    gates, uppers = refs[:6], refs[6:12]
    part, r1, r2, r3, x_ref, wg_ref, wu_ref = refs[12:19]
    acc_in = refs[19] if has_acc else None
    acc, gate_out, up_out, gate_grad, up_grad = refs[-5:]
    block, width = gates[0].shape
    ragged = rows % block != 0
    end = k_ref[1] == 1
    for slot in range(4):
        gate, upper = slot_value(end, gates, slot), slot_value(end, uppers, slot)
        j = place(k_ref, slot)
        at = columns(j, width)
        hidden_grad = (
            part[j]
            + r2[j].astype(jnp.float32)
            + jnp.where(end, r3[j], r1[j]).astype(jnp.float32)
        )
        sigma = sigmoid(gate)
        up_value = (hidden_grad * (gate * sigma)).astype(jnp.bfloat16)
        gate_value = (
            hidden_grad * upper * sigma * (1.0 + gate * (1.0 - sigma))
        ).astype(jnp.bfloat16)
        if ragged:
            up_value = valid_rows(up_value, rows, block)
            gate_value = valid_rows(gate_value, rows, block)
        up_grad[:, at] = up_value
        gate_grad[:, at] = gate_value

    @pl.when(pl.program_id(0) == 0)
    def _():
        if has_acc:
            acc[...] = acc_in[...]
        else:
            acc[...] = jnp.zeros_like(acc)

    features = x_ref.shape[1]
    step = min(features, 512)
    for c in range(0, features, step):
        cols = slice(c, c + step)
        gate_out[:, cols] = jnp.dot(
            gate_grad[...], x_ref[:, cols], preferred_element_type=jnp.float32
        ).astype(jnp.bfloat16)
        up_out[:, cols] = jnp.dot(
            up_grad[...], x_ref[:, cols], preferred_element_type=jnp.float32
        ).astype(jnp.bfloat16)
        wg, wu = wg_ref[:, cols], wu_ref[:, cols]
        if ragged:
            wg, wu = valid_rows(wg, rows, block), valid_rows(wu, rows, block)
        dims = (((0,), (0,)), ((), ()))
        acc[:, cols] += lax.dot_general(
            gate_grad[...], wg, dims, preferred_element_type=jnp.float32
        ) + lax.dot_general(
            up_grad[...], wu, dims, preferred_element_type=jnp.float32
        )


def token_kernel(rows, block, *refs):
    up_factor, gate_factor, part, r1, r2, r3, wg_ref, wu_ref, acc_in = refs[1:10]
    k_ref, (gate_out, up_out, acc, rounded, gate_grad, up_grad) = refs[0], refs[10:]
    count, _, width = part.shape
    ragged = rows % block != 0
    end = k_ref[1] == 1
    for j in range(count):
        hidden_grad = (
            part[j]
            + r2[j].astype(jnp.float32)
            + jnp.where(end, r3[j], r1[j]).astype(jnp.float32)
        )
        up_value = (hidden_grad * up_factor[j]).astype(jnp.bfloat16)
        gate_value = (hidden_grad * gate_factor[j]).astype(jnp.bfloat16)
        if ragged:
            up_value = valid_rows(up_value, rows, block)
            gate_value = valid_rows(gate_value, rows, block)
        up_out[j] = up_value
        gate_out[j] = gate_value
        up_grad[:, j * width : (j + 1) * width] = up_value
        gate_grad[:, j * width : (j + 1) * width] = gate_value

    @pl.when(pl.program_id(0) == 0)
    def _():
        acc[...] = acc_in[...]

    features = wg_ref.shape[1]
    step = min(features, 512)
    for c in range(0, features, step):
        cols = slice(c, c + step)
        wg, wu = wg_ref[:, cols], wu_ref[:, cols]
        if ragged:
            wg, wu = valid_rows(wg, rows, block), valid_rows(wu, rows, block)
        dims = (((0,), (0,)), ((), ()))
        more = lax.dot_general(
            gate_grad[...], wg, dims, preferred_element_type=jnp.float32
        ) + lax.dot_general(
            up_grad[...], wu, dims, preferred_element_type=jnp.float32
        )
        acc[:, :, cols] += more.reshape(count, width, step)

    @pl.when(pl.program_id(0) == pl.num_programs(0) - 1)
    def _():
        rounded[...] = acc[...].astype(jnp.bfloat16)


def weight_kernel(parts, *refs):
    x_ref, out_ref, grad = refs[parts], refs[-2], refs[-1]
    count, _, width = refs[0].shape
    for q in range(parts):
        for j in range(count):
            at = (j * parts + q) * width
            grad[:, at : at + width] = refs[q][j]
    features = x_ref.shape[1]
    step = min(features, 512)
    for c in range(0, features, step):
        cols = slice(c, c + step)
        out_ref[:, cols] = jnp.dot(
            grad[...], x_ref[:, cols], preferred_element_type=jnp.float32
        ).astype(jnp.bfloat16)


def once(shape):
    return pl.BlockSpec(shape, lambda i, *k: (0, 0), pipeline_mode=pl.Buffered(1))


def sum_group(w_down, grad_whole, a, size, count):
    tokens, features = grad_whole.shape
    block = block_rows(size)
    blocks = size // block
    width = tokens // count
    return pl.pallas_call(
        sum_kernel,
        grid=(blocks,),
        in_specs=[
            pl.BlockSpec((block, features), lambda i: (a * blocks + i, 0)),
            once((tokens, features)),
        ],
        out_specs=pl.BlockSpec((count, block, width), lambda i: (0, i, 0)),
        out_shape=jax.ShapeDtypeStruct((count, size, width), jnp.float32),
        compiler_params=pltpu.CompilerParams(vmem_limit_bytes=VMEM_LIMIT),
        cost_estimate=pl.CostEstimate(
            flops=2 * size * tokens * features,
            bytes_accessed=size * (features * 2 + tokens * 4),
            transcendentals=0,
        ),
    )(w_down, grad_whole)


def slot_specs(a, block, width):
    gate = pl.BlockSpec((None, block, width), lambda i, k: (a % 2, i, 0))
    upper = pl.BlockSpec((None, block, width), lambda i, k: (2 + a % 2, i, 0))
    return [gate] * 6 + [upper] * 6


def down_group(k, slots, grad_whole, out, a, size, total, factors):
    tokens, features = grad_whole.shape
    width = slots[0].shape[2]
    block = block_rows(size)
    blocks = size // block
    specs = slot_specs(a, block, width) + [once((tokens, features))]
    args = list(slots) * 2 + [grad_whole]
    aliases = {}
    if out is not None:
        aliases[1 + len(args)] = 0
        args.append(out)
        specs.append(pl.BlockSpec(memory_space=pl.ANY))
    count = slots[0].shape[0]
    wide = pl.BlockSpec((count, block, width), lambda i, k: (0, i, 0))
    factor = jax.ShapeDtypeStruct((count, size, width), jnp.float32)
    return pl.pallas_call(
        functools.partial(down_kernel, factors),
        grid_spec=pltpu.PrefetchScalarGridSpec(
            num_scalar_prefetch=1,
            grid=(blocks,),
            in_specs=specs,
            out_specs=[
                pl.BlockSpec((block, features), lambda i, k: (a * blocks + i, 0))
            ]
            + [wide] * (2 * factors),
            scratch_shapes=[pltpu.VMEM((block, tokens), jnp.bfloat16)],
        ),
        out_shape=[jax.ShapeDtypeStruct((total, features), jnp.bfloat16)]
        + [factor] * (2 * factors),
        input_output_aliases=aliases,
        compiler_params=pltpu.CompilerParams(vmem_limit_bytes=VMEM_LIMIT),
        cost_estimate=pl.CostEstimate(
            flops=2 * size * tokens * features,
            bytes_accessed=size * (features * 2 + tokens * 4),
            transcendentals=size * tokens,
        ),
    )(k, *args)


def main_group(k, slots, sums, x_whole, wg, wu, acc, outs, a, size, total):
    tokens, features = x_whole.shape
    count, _, width = slots[0].shape
    block = block_rows(size)
    blocks = size // block
    wide = pl.BlockSpec((count, block, width), lambda i, k: (0, i, 0))
    weight = pl.BlockSpec((block, features), lambda i, k: (a * blocks + i, 0))
    specs = (
        slot_specs(a, block, width)
        + [wide] * 4
        + [once((tokens, features)), weight, weight]
    )
    args = list(slots) * 2 + list(sums) + [x_whole, wg, wu]
    aliases = {}
    if acc is not None:
        aliases[1 + len(args)] = 0
        args.append(acc)
        specs.append(once((tokens, features)))
        for i, out in enumerate(outs):
            aliases[1 + len(args)] = 1 + i
            args.append(out)
            specs.append(pl.BlockSpec(memory_space=pl.ANY))
    wgrad = jax.ShapeDtypeStruct((total, features), jnp.bfloat16)
    rows = min(size, total - a * size)
    return pl.pallas_call(
        functools.partial(main_kernel, rows, acc is not None),
        grid_spec=pltpu.PrefetchScalarGridSpec(
            num_scalar_prefetch=1,
            grid=(blocks,),
            in_specs=specs,
            out_specs=(once((tokens, features)), weight, weight),
            scratch_shapes=[pltpu.VMEM((block, tokens), jnp.bfloat16)] * 2,
        ),
        out_shape=(
            jax.ShapeDtypeStruct((tokens, features), jnp.float32),
            wgrad,
            wgrad,
        ),
        input_output_aliases=aliases,
        compiler_params=pltpu.CompilerParams(vmem_limit_bytes=VMEM_LIMIT),
        cost_estimate=pl.CostEstimate(
            flops=8 * size * tokens * features,
            bytes_accessed=size * (features * 8 + tokens * 14),
            transcendentals=size * tokens,
        ),
    )(k, *args)


def token_group(k, factors, sums, r3, wg, wu, acc, q, a, size, total):
    tokens, features = acc.shape
    count, _, width = r3.shape
    block = block_rows(size)
    blocks = size // block
    parts = tokens // (count * width)

    def split(value):
        return value.reshape((count, parts) + value.shape[1:])

    some = pl.BlockSpec((count, None, block, width), lambda i, k: (0, q, i, 0))
    wide = pl.BlockSpec((count, block, width), lambda i, k: (0, i, 0))
    weight = pl.BlockSpec((block, features), lambda i, k: (a * blocks + i, 0))
    rows = min(size, total - a * size)
    grad = jax.ShapeDtypeStruct((count, size, width), jnp.bfloat16)
    whole = pl.BlockSpec(
        (count, width, features),
        lambda i, k: (0, 0, 0),
        pipeline_mode=pl.Buffered(1),
    )
    return pl.pallas_call(
        functools.partial(token_kernel, rows, block),
        grid_spec=pltpu.PrefetchScalarGridSpec(
            num_scalar_prefetch=1,
            grid=(blocks,),
            in_specs=[some] * 5
            + [wide, weight, weight]
            + [
                pl.BlockSpec(
                    (count, None, width, features),
                    lambda i, k: (0, q, 0, 0),
                    pipeline_mode=pl.Buffered(1),
                )
            ],
            out_specs=[wide, wide, whole, whole],
            scratch_shapes=[pltpu.VMEM((block, count * width), jnp.bfloat16)] * 2,
        ),
        out_shape=[
            grad,
            grad,
            jax.ShapeDtypeStruct((count, width, features), jnp.float32),
            jax.ShapeDtypeStruct((count, width, features), jnp.bfloat16),
        ],
        compiler_params=pltpu.CompilerParams(vmem_limit_bytes=VMEM_LIMIT),
        cost_estimate=pl.CostEstimate(
            flops=4 * size * count * width * features,
            bytes_accessed=size * (features * 4 + count * width * 22),
            transcendentals=0,
        ),
    )(
        k,
        *[split(f) for f in factors],
        *[split(s) for s in sums],
        r3,
        wg,
        wu,
        acc.reshape(count, parts, width, features),
    )


def weight_group(grads, x_whole, out, a, size):
    tokens, features = x_whole.shape
    count, _, width = grads[0].shape
    block = block_rows(size)
    blocks = size // block
    wide = pl.BlockSpec((count, block, width), lambda i: (0, i, 0))
    return pl.pallas_call(
        functools.partial(weight_kernel, len(grads)),
        grid=(blocks,),
        in_specs=[wide] * len(grads)
        + [once((tokens, features)), pl.BlockSpec(memory_space=pl.ANY)],
        out_specs=pl.BlockSpec((block, features), lambda i: (a * blocks + i, 0)),
        scratch_shapes=[pltpu.VMEM((block, tokens), jnp.bfloat16)],
        out_shape=jax.ShapeDtypeStruct(out.shape, out.dtype),
        input_output_aliases={len(grads) + 1: 0},
        compiler_params=pltpu.CompilerParams(vmem_limit_bytes=VMEM_LIMIT),
        cost_estimate=pl.CostEstimate(
            flops=2 * size * tokens * features,
            bytes_accessed=size * (features * 2 + tokens * 2),
            transcendentals=0,
        ),
    )(*grads, x_whole, out)


def halve(value, axis, bit, mine, pairs):
    size = value.shape[axis]
    shape = value.shape
    view = value.reshape(shape[:axis] + (size // (2 * bit), 2, bit) + shape[axis + 1 :])
    away = lax.dynamic_index_in_dim(view, 1 - mine, axis + 1, keepdims=False)
    kept = lax.dynamic_index_in_dim(view, mine, axis + 1, keepdims=False)
    rest = shape[:axis] + (size // 2,) + shape[axis + 1 :]
    got = lax.ppermute(away.reshape(rest).astype(jnp.bfloat16), ("wt", "dep"), pairs)
    return kept.reshape(rest) + got.astype(jnp.float32)


def scatter_half(value, rounded, q, n_wt, n_dep):
    at_wt, at_dep = lax.axis_index("wt"), lax.axis_index("dep")

    def pairs(bit_wt, bit_dep):
        return [
            (w * n_dep + d, (w ^ bit_wt) * n_dep + (d ^ bit_dep))
            for w in range(n_wt)
            for d in range(n_dep)
            if w % 2 == q
        ]

    inward = [
        (w * n_dep + d, (w ^ 1) * n_dep + d)
        for w in range(n_wt)
        for d in range(n_dep)
        if w % 2 != q
    ]
    features = value.shape[-1]
    blocks = (n_wt // 2, n_dep, -1, features)
    value = value.reshape(blocks)
    got = lax.ppermute(rounded, ("wt", "dep"), inward).reshape(blocks)

    def over_wt(part):
        bit = 2
        while bit < n_wt:
            mine = (at_wt // bit) % 2
            part = halve(part, 0, 1, mine, pairs(bit, 0))
            bit *= 2
        return part

    def over_dep(part):
        bit = 1
        while bit < n_dep:
            mine = (at_dep // bit) % 2
            part = halve(part, 1, 1, mine, pairs(0, bit))
            bit *= 2
        return part

    half = features // 2
    one = value[..., :half] + got[..., :half].astype(jnp.float32)
    two = value[..., half:] + got[..., half:].astype(jnp.float32)
    one, two = over_dep(over_wt(one)), over_wt(over_dep(two))
    return jnp.concatenate([one[0, 0], two[0, 0]], axis=-1)


def own_half(gate, upper, half, size):
    first, last = 2 * half * size, 2 * (half + 1) * size
    parts = []
    for whole in (gate, upper):
        part = whole[first : min(last, whole.shape[0])]
        part = jnp.pad(part, ((0, last - first - part.shape[0]), (0, 0)))
        parts.append(part.reshape(2, size, -1))
    return jnp.concatenate(parts, axis=0)


def per_device(n_wt, n_dep, x_saved, out_grad, gate_pre, up_pre, w_gate, w_up, w_down):
    index = lax.axis_index("inp")
    end = (index == 0) | (index == 3)
    k = jnp.stack([index, end]).astype(jnp.int32)
    total = w_down.shape[0]
    size = 16 * -(-total // (16 * GROUPS))
    gate, upper = gate_pre.T, up_pre.T
    wg, wu = w_gate.T, w_up.T

    def rounded(part, got):
        return (part + got.astype(jnp.float32)).astype(jnp.bfloat16)

    own = [own_half(gate, upper, half, size) for half in range(2)]
    swap, middle = [], []
    for step in range(2):
        swap.append(send(own[step], SWAP))
        middle.append(send(own[step], MIDDLE))
    x_whole, grad_whole = (
        lax.all_gather(x_saved, ("wt", "dep"), axis=0, tiled=True),
        lax.all_gather(out_grad, ("wt", "dep"), axis=0, tiled=True),
    )
    part = [sum_group(w_down, grad_whole, a, size, 4) for a in range(GROUPS)]
    down = None
    acc, wgrads = None, (None, None)
    last = GROUPS - 1
    factors = None

    def slots_of(a):
        h = a // 2
        return [own[h], swap[h], swap[2 + h], middle[2 + h], swap[4 + h], middle[h]]

    for step in range(2, 10):
        if step < 4:
            swap[step - 2] = tie(swap[step - 2], part[step - 2])
            middle.append(send(swap[step - 2], MIDDLE))
        if step < 6:
            outward = part[step - 2].astype(jnp.bfloat16)
            payload = jnp.where(end, outward, middle[step - 2])
            swap.append(send(payload, SWAP))
        elif step < 9:
            payload = rounded(part[step - 6], middle[step - 2])
            if step == 8:
                payload = tie(payload, swap[6], down)
            swap.append(send(payload, TO_ENDS))
        if 4 <= step < 8:
            middle.append(send(rounded(part[step - 4], swap[step - 2]), MIDDLE))
        if step == 6 or step == 7:
            for a in (2 * step - 12, 2 * step - 11):
                down, *factors = down_group(
                    k, slots_of(a), grad_whole, down, a, size, total, a == last
                )

    def main(a, acc, wgrads):
        sums = [part[a], swap[2 + a], middle[4 + a], swap[6 + a]]
        acc, *wgrads = main_group(
            k, slots_of(a), sums, x_whole, wg, wu, acc, wgrads, a, size, total
        )
        return acc, wgrads

    def pieces(value):
        return value.reshape((2, 2) + value.shape[1:])

    final = []
    for q in range(2):
        payload = rounded(pieces(part[last])[:, q], pieces(middle[4 + last])[:, q])
        if q == 0:
            payload = tie(payload, swap[7])
        else:
            acc, wgrads = main(0, acc, wgrads)
            payload = tie(payload, acc)
        final.append(send(payload, TO_ENDS))
    for a in range(1, last):
        acc, wgrads = main(a, acc, wgrads)
    sums = [part[last], swap[2 + last], middle[4 + last]]
    gate_grads, up_grads, shares = [], [], []
    for q in range(2):
        gate_part, up_part, value, small = token_group(
            k, factors, sums, final[q], wg, wu, acc, q, last, size, total
        )
        gate_grads.append(gate_part)
        up_grads.append(up_part)
        shares.append(scatter_half(value, small, q, n_wt, n_dep))
    gate_wgrad = weight_group(gate_grads, x_whole, wgrads[0], last, size)
    up_wgrad = weight_group(up_grads, x_whole, wgrads[1], last, size)
    input_grad = jnp.where(lax.axis_index("wt") % 2 == 0, *shares)
    return (input_grad.astype(jnp.bfloat16), gate_wgrad.T, up_wgrad.T, down)


def solution(mesh):
    placed = (
        P(("wt", "dep"), "inp"),
        P(("wt", "dep"), "inp"),
        P("inp", ("wt", "dep")),
        P("inp", ("wt", "dep")),
        P("inp", ("wt", "dep")),
        P("inp", ("wt", "dep")),
        P(("wt", "dep"), "inp"),
    )
    return jax.shard_map(
        functools.partial(per_device, mesh.shape["wt"], mesh.shape["dep"]),
        mesh=mesh,
        in_specs=placed,
        out_specs=(
            P(("wt", "dep"), "inp"),
            P("inp", ("wt", "dep")),
            P("inp", ("wt", "dep")),
            P(("wt", "dep"), "inp"),
        ),
        check_vma=False,
    )
```

```python
import functools

import jax
import jax.numpy as jnp
from jax import lax
from jax.experimental import pallas as pl
from jax.experimental.pallas import tpu as pltpu
from jax.sharding import PartitionSpec as P

GROUPS = 4
VMEM_LIMIT = 60 * 1024 * 1024

SWAP = [(0, 1), (1, 0), (2, 3), (3, 2)]
MIDDLE = [(1, 2), (2, 1)]
TO_ENDS = [(1, 0), (2, 3)]


def tie(value, *after):
    return pl.pallas_call(
        lambda *refs: None,
        in_specs=[pl.BlockSpec(memory_space=pl.ANY)] * (1 + len(after)),
        out_specs=pl.BlockSpec(memory_space=pl.ANY),
        out_shape=jax.ShapeDtypeStruct(value.shape, value.dtype),
        input_output_aliases={0: 0},
    )(value, *after)


def send(value, pairs):
    return lax.ppermute(value, "inp", pairs)


def block_rows(rows):
    units = rows // 16
    return 16 * max(n for n in range(1, 33) if units % n == 0)


def sum_kernel(w_ref, grad_ref, out_ref):
    count, _, width = out_ref.shape
    for j in range(count):
        out_ref[j] = lax.dot_general(
            w_ref[...],
            grad_ref[j * width : (j + 1) * width, :],
            (((1,), (1,)), ((), ())),
            preferred_element_type=jnp.float32,
        )


def sigmoid(value):
    return 0.5 + 0.5 * jnp.tanh(0.5 * value)


def slot_value(end, refs, slot):
    if slot == 0:
        return refs[0][...].astype(jnp.float32)
    if slot == 1:
        return refs[1][...].astype(jnp.float32)
    at_end, at_middle = refs[2:4] if slot == 2 else refs[4:6]
    return jnp.where(end, at_end[...], at_middle[...]).astype(jnp.float32)


def place(k_ref, slot):
    return k_ref[0] ^ slot


def columns(index, width):
    return pl.ds(pl.multiple_of(index * width, width), width)


def down_kernel(factors, k_ref, *refs):
    gates, uppers = refs[:6], refs[6:12]
    grad_ref, hidden = refs[12], refs[-1]
    out_ref = refs[-4] if factors else refs[-2]
    width = gates[0].shape[1]
    end = k_ref[1] == 1
    for slot in range(4):
        gate, upper = slot_value(end, gates, slot), slot_value(end, uppers, slot)
        j = place(k_ref, slot)
        sigma = sigmoid(gate)
        active = gate * sigma
        hidden[:, columns(j, width)] = (active * upper).astype(jnp.bfloat16)
        if factors:
            refs[-3][j] = active
            refs[-2][j] = upper * sigma * (1.0 + gate * (1.0 - sigma))
    features = grad_ref.shape[1]
    step = min(features, 512)
    for c in range(0, features, step):
        cols = slice(c, c + step)
        out_ref[:, cols] = jnp.dot(
            hidden[...], grad_ref[:, cols], preferred_element_type=jnp.float32
        ).astype(jnp.bfloat16)


def main_kernel(has_acc, k_ref, *refs):
    gates, uppers = refs[:6], refs[6:12]
    part, r1, r2, r3, x_hbm, wg_ref, wu_ref = refs[12:19]
    acc_in = refs[19] if has_acc else None
    acc_out, gate_out, up_out = refs[-11:-8]
    gate_grad, up_grad, gate_turned, up_turned, x_ref, acc, sems, out_sems = refs[-8:]
    block, width = gates[0].shape
    end = k_ref[1] == 1
    first = pl.program_id(0) == 0
    x_copy = pltpu.make_async_copy(x_hbm, x_ref, sems.at[0])
    acc_copy = pltpu.make_async_copy(acc_in, acc, sems.at[1]) if has_acc else None

    @pl.when(first)
    def _():
        x_copy.start()
        if has_acc:
            acc_copy.start()
        else:
            acc[...] = jnp.zeros_like(acc)

    for slot in range(4):
        gate, upper = slot_value(end, gates, slot), slot_value(end, uppers, slot)
        j = place(k_ref, slot)
        at = columns(j, width)
        hidden_grad = (
            part[j]
            + r2[j].astype(jnp.float32)
            + jnp.where(end, r3[j], r1[j]).astype(jnp.float32)
        )
        sigma = sigmoid(gate)
        up_value = (hidden_grad * (gate * sigma)).astype(jnp.bfloat16)
        gate_value = (
            hidden_grad * upper * sigma * (1.0 + gate * (1.0 - sigma))
        ).astype(jnp.bfloat16)
        up_grad[:, at] = up_value
        gate_grad[:, at] = gate_value
        up_turned[at, :] = up_value.T
        gate_turned[at, :] = gate_value.T

    features = x_ref.shape[1]
    step = min(features, 512)
    tiles = [slice(c, c + step) for c in range(0, features, step)]

    @pl.when(first)
    def _():
        x_copy.wait()

    for cols in tiles:
        gate_out[:, cols] = jnp.dot(
            gate_grad[...], x_ref[:, cols], preferred_element_type=jnp.float32
        ).astype(jnp.bfloat16)

    if has_acc:

        @pl.when(first)
        def _():
            acc_copy.wait()

    last = pl.program_id(0) == pl.num_programs(0) - 1
    out_copies = [
        pltpu.make_async_copy(acc.at[:, cols], acc_out.at[:, cols], out_sems.at[i])
        for i, cols in enumerate(tiles)
    ]
    for i, cols in enumerate(tiles):
        acc[:, cols] += jnp.dot(
            gate_turned[...], wg_ref[:, cols], preferred_element_type=jnp.float32
        ) + jnp.dot(
            up_turned[...], wu_ref[:, cols], preferred_element_type=jnp.float32
        )
        pl.when(last)(out_copies[i].start)

    for cols in tiles:
        up_out[:, cols] = jnp.dot(
            up_grad[...], x_ref[:, cols], preferred_element_type=jnp.float32
        ).astype(jnp.bfloat16)

    @pl.when(last)
    def _():
        for copy in out_copies:
            copy.wait()


def token_kernel(rows, *refs):
    up_factor, gate_factor, part, r1, r2, r3, wg_ref, wu_ref, acc_in = refs[1:10]
    k_ref, (gate_out, up_out, acc, rounded, gate_grad, up_grad) = refs[0], refs[10:]
    count, size, width = part.shape
    ragged = rows < size
    end = k_ref[1] == 1

    def valid(value):
        if not ragged:
            return value
        at = lax.broadcasted_iota(jnp.int32, value.shape, 0)
        return jnp.where(at < rows, value, jnp.zeros_like(value))

    @pl.when(pl.program_id(0) == 0)
    def _():
        for j in range(count):
            hidden_grad = (
                part[j]
                + r2[j].astype(jnp.float32)
                + jnp.where(end, r3[j], r1[j]).astype(jnp.float32)
            )
            up_value = valid((hidden_grad * up_factor[j]).astype(jnp.bfloat16))
            gate_value = valid((hidden_grad * gate_factor[j]).astype(jnp.bfloat16))
            up_out[j] = up_value
            gate_out[j] = gate_value
            up_grad[j * width : (j + 1) * width, :] = up_value.T
            gate_grad[j * width : (j + 1) * width, :] = gate_value.T

    more = jnp.dot(
        gate_grad[...], valid(wg_ref[...]), preferred_element_type=jnp.float32
    ) + jnp.dot(up_grad[...], valid(wu_ref[...]), preferred_element_type=jnp.float32)
    value = acc_in[...] + more.reshape(acc.shape)
    acc[...] = value
    rounded[...] = value.astype(jnp.bfloat16)


def weight_kernel(parts, *refs):
    x_ref, out_ref, grad = refs[parts], refs[-2], refs[-1]
    count, _, width = refs[0].shape
    for q in range(parts):
        for j in range(count):
            at = (j * parts + q) * width
            grad[:, at : at + width] = refs[q][j]
    features = x_ref.shape[1]
    step = min(features, 512)
    for c in range(0, features, step):
        cols = slice(c, c + step)
        out_ref[:, cols] = jnp.dot(
            grad[...], x_ref[:, cols], preferred_element_type=jnp.float32
        ).astype(jnp.bfloat16)


def once(shape):
    return pl.BlockSpec(shape, lambda i, *k: (0, 0), pipeline_mode=pl.Buffered(1))


def sum_group(w_down, grad_whole, a, size, count):
    tokens, features = grad_whole.shape
    block = block_rows(size)
    blocks = size // block
    width = tokens // count
    return pl.pallas_call(
        sum_kernel,
        grid=(blocks,),
        in_specs=[
            pl.BlockSpec((block, features), lambda i: (a * blocks + i, 0)),
            once((tokens, features)),
        ],
        out_specs=pl.BlockSpec((count, block, width), lambda i: (0, i, 0)),
        out_shape=jax.ShapeDtypeStruct((count, size, width), jnp.float32),
        compiler_params=pltpu.CompilerParams(vmem_limit_bytes=VMEM_LIMIT),
        cost_estimate=pl.CostEstimate(
            flops=2 * size * tokens * features,
            bytes_accessed=size * (features * 2 + tokens * 4),
            transcendentals=0,
        ),
    )(w_down, grad_whole)


def slot_specs(a, block, width, at=0):
    gate = pl.BlockSpec((None, block, width), lambda i, k: (a % 2, at + i, 0))
    upper = pl.BlockSpec((None, block, width), lambda i, k: (2 + a % 2, at + i, 0))
    return [gate] * 6 + [upper] * 6


def down_group(k, slots, grad_whole, out, a, size, total, factors):
    tokens, features = grad_whole.shape
    width = slots[0].shape[2]
    block = block_rows(size)
    blocks = size // block
    specs = slot_specs(a, block, width) + [once((tokens, features))]
    args = list(slots) * 2 + [grad_whole]
    aliases = {}
    if out is not None:
        aliases[1 + len(args)] = 0
        args.append(out)
        specs.append(pl.BlockSpec(memory_space=pl.ANY))
    count = slots[0].shape[0]
    wide = pl.BlockSpec((count, block, width), lambda i, k: (0, i, 0))
    factor = jax.ShapeDtypeStruct((count, size, width), jnp.float32)
    return pl.pallas_call(
        functools.partial(down_kernel, factors),
        grid_spec=pltpu.PrefetchScalarGridSpec(
            num_scalar_prefetch=1,
            grid=(blocks,),
            in_specs=specs,
            out_specs=[
                pl.BlockSpec((block, features), lambda i, k: (a * blocks + i, 0))
            ]
            + [wide] * (2 * factors),
            scratch_shapes=[pltpu.VMEM((block, tokens), jnp.bfloat16)],
        ),
        out_shape=[jax.ShapeDtypeStruct((total, features), jnp.bfloat16)]
        + [factor] * (2 * factors),
        input_output_aliases=aliases,
        compiler_params=pltpu.CompilerParams(vmem_limit_bytes=VMEM_LIMIT),
        cost_estimate=pl.CostEstimate(
            flops=2 * size * tokens * features,
            bytes_accessed=size * (features * 2 + tokens * 4),
            transcendentals=size * tokens,
        ),
    )(k, *args)


def main_group(k, slots, sums, r3, x_whole, wg, wu, acc, outs, a, run, size, total):
    tokens, features = x_whole.shape
    count, _, width = slots[0].shape
    block = block_rows(size)
    base = a * (size // block) + run[0]
    blocks = run[1] - run[0]
    wide = pl.BlockSpec((count, block, width), lambda i, k: (0, run[0] + i, 0))
    weight = pl.BlockSpec((block, features), lambda i, k: (base + i, 0))
    specs = (
        slot_specs(a, block, width, run[0])
        + [wide] * 3
        + [pl.BlockSpec((count, block, width), lambda i, k: (0, i, 0))]
        + [pl.BlockSpec(memory_space=pl.ANY), weight, weight]
    )
    args = list(slots) * 2 + list(sums) + [r3, x_whole, wg, wu]
    aliases = {}
    if acc is not None:
        aliases[1 + len(args)] = 0
        args.append(acc)
        specs.append(pl.BlockSpec(memory_space=pl.ANY))
        for i, out in enumerate(outs):
            aliases[1 + len(args)] = 1 + i
            args.append(out)
            specs.append(pl.BlockSpec(memory_space=pl.ANY))
    wgrad = jax.ShapeDtypeStruct((total, features), jnp.bfloat16)
    size = blocks * block
    return pl.pallas_call(
        functools.partial(main_kernel, acc is not None),
        grid_spec=pltpu.PrefetchScalarGridSpec(
            num_scalar_prefetch=1,
            grid=(blocks,),
            in_specs=specs,
            out_specs=(pl.BlockSpec(memory_space=pl.ANY), weight, weight),
            scratch_shapes=[pltpu.VMEM((block, tokens), jnp.bfloat16)] * 2
            + [pltpu.VMEM((tokens, block), jnp.bfloat16)] * 2
            + [
                pltpu.VMEM((tokens, features), jnp.bfloat16),
                pltpu.VMEM((tokens, features), jnp.float32),
                pltpu.SemaphoreType.DMA((2,)),
                pltpu.SemaphoreType.DMA((-(-features // min(features, 512)),)),
            ],
        ),
        out_shape=(
            jax.ShapeDtypeStruct((tokens, features), jnp.float32),
            wgrad,
            wgrad,
        ),
        input_output_aliases=aliases,
        compiler_params=pltpu.CompilerParams(vmem_limit_bytes=VMEM_LIMIT),
        cost_estimate=pl.CostEstimate(
            flops=8 * size * tokens * features,
            bytes_accessed=size * (features * 8 + tokens * 14),
            transcendentals=size * tokens,
        ),
    )(k, *args)


def token_group(k, factors, sums, r3, wg, wu, acc, q, a, size, total):
    tokens, features = acc.shape
    count, _, width = r3.shape
    step = min(features, 512)
    parts = tokens // (count * width)

    def split(value):
        return value.reshape((count, parts) + value.shape[1:])

    kept = pl.Buffered(1)
    some = pl.BlockSpec(
        (count, None, size, width), lambda i, k: (0, q, 0, 0), pipeline_mode=kept
    )
    wide = pl.BlockSpec(
        (count, size, width), lambda i, k: (0, 0, 0), pipeline_mode=kept
    )
    weight = pl.BlockSpec((size, step), lambda i, k: (a, i))
    rows = min(size, total - a * size)
    grad = jax.ShapeDtypeStruct((count, size, width), jnp.bfloat16)
    whole = pl.BlockSpec((count, width, step), lambda i, k: (0, 0, i))
    return pl.pallas_call(
        functools.partial(token_kernel, rows),
        grid_spec=pltpu.PrefetchScalarGridSpec(
            num_scalar_prefetch=1,
            grid=(-(-features // step),),
            in_specs=[some] * 5
            + [wide, weight, weight]
            + [
                pl.BlockSpec(
                    (count, None, width, step), lambda i, k: (0, q, 0, i)
                )
            ],
            out_specs=[wide, wide, whole, whole],
            scratch_shapes=[pltpu.VMEM((count * width, size), jnp.bfloat16)] * 2,
        ),
        out_shape=[
            grad,
            grad,
            jax.ShapeDtypeStruct((count, width, features), jnp.float32),
            jax.ShapeDtypeStruct((count, width, features), jnp.bfloat16),
        ],
        compiler_params=pltpu.CompilerParams(vmem_limit_bytes=VMEM_LIMIT),
        cost_estimate=pl.CostEstimate(
            flops=4 * size * count * width * features,
            bytes_accessed=size * (features * 4 + count * width * 22),
            transcendentals=0,
        ),
    )(
        k,
        *[split(f) for f in factors],
        *[split(s) for s in sums],
        r3,
        wg,
        wu,
        acc.reshape(count, parts, width, features),
    )


def weight_group(grads, x_whole, out, a, size, after):
    tokens, features = x_whole.shape
    count, _, width = grads[0].shape
    block = block_rows(size)
    blocks = size // block
    wide = pl.BlockSpec((count, block, width), lambda i: (0, i, 0))
    return pl.pallas_call(
        functools.partial(weight_kernel, len(grads)),
        grid=(blocks,),
        in_specs=[wide] * len(grads)
        + [once((tokens, features)), pl.BlockSpec(memory_space=pl.ANY)]
        + [pl.BlockSpec(memory_space=pl.ANY)] * len(after),
        out_specs=pl.BlockSpec((block, features), lambda i: (a * blocks + i, 0)),
        scratch_shapes=[pltpu.VMEM((block, tokens), jnp.bfloat16)],
        out_shape=jax.ShapeDtypeStruct(out.shape, out.dtype),
        input_output_aliases={len(grads) + 1: 0},
        compiler_params=pltpu.CompilerParams(vmem_limit_bytes=VMEM_LIMIT),
        cost_estimate=pl.CostEstimate(
            flops=2 * size * tokens * features,
            bytes_accessed=size * (features * 2 + tokens * 2),
            transcendentals=0,
        ),
    )(*grads, x_whole, out, *after)


def halve(value, axis, bit, mine, pairs):
    size = value.shape[axis]
    shape = value.shape
    view = value.reshape(shape[:axis] + (size // (2 * bit), 2, bit) + shape[axis + 1 :])
    away = lax.dynamic_index_in_dim(view, 1 - mine, axis + 1, keepdims=False)
    kept = lax.dynamic_index_in_dim(view, mine, axis + 1, keepdims=False)
    rest = shape[:axis] + (size // 2,) + shape[axis + 1 :]
    got = lax.ppermute(away.reshape(rest).astype(jnp.bfloat16), ("wt", "dep"), pairs)
    return kept.reshape(rest) + got.astype(jnp.float32)


def scatter_half(value, rounded, q, n_wt, n_dep):
    at_wt, at_dep = lax.axis_index("wt"), lax.axis_index("dep")

    def pairs(bit_wt, bit_dep):
        return [
            (w * n_dep + d, (w ^ bit_wt) * n_dep + (d ^ bit_dep))
            for w in range(n_wt)
            for d in range(n_dep)
            if w % 2 == q
        ]

    inward = [
        (w * n_dep + d, (w ^ 1) * n_dep + d)
        for w in range(n_wt)
        for d in range(n_dep)
        if w % 2 != q
    ]
    features = value.shape[-1]
    blocks = (n_wt // 2, n_dep, -1, features)
    value = value.reshape(blocks)
    first = lax.ppermute(rounded, ("wt", "dep"), inward)
    got = first.reshape(blocks)

    def over_wt(part):
        bit = 2
        while bit < n_wt:
            mine = (at_wt // bit) % 2
            part = halve(part, 0, 1, mine, pairs(bit, 0))
            bit *= 2
        return part

    def over_dep(part):
        bit = 1
        while bit < n_dep:
            mine = (at_dep // bit) % 2
            part = halve(part, 1, 1, mine, pairs(0, bit))
            bit *= 2
        return part

    half = features // 2
    one = value[..., :half] + got[..., :half].astype(jnp.float32)
    two = value[..., half:] + got[..., half:].astype(jnp.float32)
    one, two = over_wt(one), over_dep(two)
    stages = [first, one]
    one, two = over_dep(one), over_wt(two)
    return jnp.concatenate([one[0, 0], two[0, 0]], axis=-1), stages


def own_half(gate, upper, half, size):
    first, last = 2 * half * size, 2 * (half + 1) * size
    parts = []
    for whole in (gate, upper):
        part = whole[first : min(last, whole.shape[0])]
        part = jnp.pad(part, ((0, last - first - part.shape[0]), (0, 0)))
        parts.append(part.reshape(2, size, -1))
    return jnp.concatenate(parts, axis=0)


def per_device(n_wt, n_dep, x_saved, out_grad, gate_pre, up_pre, w_gate, w_up, w_down):
    index = lax.axis_index("inp")
    end = (index == 0) | (index == 3)
    k = jnp.stack([index, end]).astype(jnp.int32)
    total = w_down.shape[0]
    size = 16 * -(-total // (16 * GROUPS))
    gate, upper = gate_pre.T, up_pre.T
    wg, wu = w_gate.T, w_up.T

    def rounded(part, got):
        return (part + got.astype(jnp.float32)).astype(jnp.bfloat16)

    own = [own_half(gate, upper, half, size) for half in range(2)]
    swap, middle = [], []
    for step in range(2):
        swap.append(send(own[step], SWAP))
        middle.append(send(own[step], MIDDLE))
    x_whole, grad_whole = (
        lax.all_gather(x_saved, ("wt", "dep"), axis=0, tiled=True),
        lax.all_gather(out_grad, ("wt", "dep"), axis=0, tiled=True),
    )
    part = [sum_group(w_down, grad_whole, a, size, 4) for a in range(GROUPS)]
    down = None
    acc, wgrads = None, (None, None)
    last = GROUPS - 1
    factors = None

    def slots_of(a):
        h = a // 2
        return [own[h], swap[h], swap[2 + h], middle[2 + h], swap[4 + h], middle[h]]

    for step in range(2, 10):
        if step < 4:
            swap[step - 2] = tie(swap[step - 2], part[step - 2])
            middle.append(send(swap[step - 2], MIDDLE))
        if step < 6:
            outward = part[step - 2].astype(jnp.bfloat16)
            payload = jnp.where(end, outward, middle[step - 2])
            swap.append(send(payload, SWAP))
        elif step < 8:
            payload = rounded(part[step - 6], middle[step - 2])
            if step == 7:
                payload = tie(payload, down)
            swap.append(send(payload, TO_ENDS))
        if 4 <= step < 8:
            middle.append(send(rounded(part[step - 4], swap[step - 2]), MIDDLE))
        if step == 6 or step == 7:
            for a in (2 * step - 12, 2 * step - 11):
                down, *factors = down_group(
                    k, slots_of(a), grad_whole, down, a, size, total, a == last
                )

    block = block_rows(size)
    blocks = size // block
    halves = [(0, blocks // 2), (blocks // 2, blocks)]
    halves = [run for run in halves if run[0] < run[1]]

    def main(a, run, r3, acc, wgrads):
        sums = [part[a], swap[2 + a], middle[4 + a]]
        args = (k, slots_of(a), sums, r3, x_whole, wg, wu, acc, wgrads)
        acc, *wgrads = main_group(*args, a, run, size, total)
        return acc, wgrads

    def pieces(value):
        return value.reshape((2, 2) + value.shape[1:])

    inner = []
    for i, run in enumerate(halves):
        rows = slice(run[0] * block, run[1] * block)
        payload = rounded(part[2][:, rows], middle[6][:, rows])
        payload = tie(payload, swap[6], down) if i == 0 else tie(payload, inner[0][1])
        inner.append((run, payload, send(payload, TO_ENDS)))
    acc, wgrads = main(0, (0, blocks), swap[6], acc, wgrads)
    final = []
    for q in range(2):
        payload = rounded(pieces(part[last])[:, q], pieces(middle[4 + last])[:, q])
        if q == 1:
            acc, wgrads = main(1, (0, blocks), swap[7], acc, wgrads)
        payload = tie(payload, swap[7], acc)
        final.append(send(payload, TO_ENDS))
    for run, _, r3 in inner:
        acc, wgrads = main(2, run, r3, acc, wgrads)
    sums = [part[last], swap[2 + last], middle[4 + last]]
    gate_grads, up_grads, shares, arrived = [], [], [], []
    for q in range(2):
        gate_part, up_part, value, small = token_group(
            k, factors, sums, final[q], wg, wu, acc, q, last, size, total
        )
        gate_grads.append(gate_part)
        up_grads.append(up_part)
        share, stages = scatter_half(value, small, q, n_wt, n_dep)
        shares.append(share)
        arrived.append(stages)
    behind = [arrived[0][0]], [arrived[0][1], arrived[1][1]]
    gate_wgrad, up_wgrad = (
        weight_group(grads, x_whole, out, last, size, after)
        for grads, out, after in zip((gate_grads, up_grads), wgrads, behind)
    )
    input_grad = jnp.where(lax.axis_index("wt") % 2 == 0, *shares)
    return (input_grad.astype(jnp.bfloat16), gate_wgrad.T, up_wgrad.T, down)


def solution(mesh):
    placed = (
        P(("wt", "dep"), "inp"),
        P(("wt", "dep"), "inp"),
        P("inp", ("wt", "dep")),
        P("inp", ("wt", "dep")),
        P("inp", ("wt", "dep")),
        P("inp", ("wt", "dep")),
        P(("wt", "dep"), "inp"),
    )
    return jax.shard_map(
        functools.partial(per_device, mesh.shape["wt"], mesh.shape["dep"]),
        mesh=mesh,
        in_specs=placed,
        out_specs=(
            P(("wt", "dep"), "inp"),
            P("inp", ("wt", "dep")),
            P("inp", ("wt", "dep")),
            P(("wt", "dep"), "inp"),
        ),
        check_vma=False,
    )
```

```python
import functools

import jax
import jax.numpy as jnp
from jax import lax
from jax.experimental import pallas as pl
from jax.experimental.pallas import tpu as pltpu
from jax.sharding import PartitionSpec as P

GROUPS = 4
VMEM_LIMIT = 60 * 1024 * 1024

SWAP = [(0, 1), (1, 0), (2, 3), (3, 2)]
MIDDLE = [(1, 2), (2, 1)]
TO_ENDS = [(1, 0), (2, 3)]


def tie(value, *after):
    return pl.pallas_call(
        lambda *refs: None,
        in_specs=[pl.BlockSpec(memory_space=pl.ANY)] * (1 + len(after)),
        out_specs=pl.BlockSpec(memory_space=pl.ANY),
        out_shape=jax.ShapeDtypeStruct(value.shape, value.dtype),
        input_output_aliases={0: 0},
    )(value, *after)


def send(value, pairs):
    return lax.ppermute(value, "inp", pairs)


def block_rows(rows):
    units = rows // 16
    return 16 * max(n for n in range(1, 33) if units % n == 0)


def sum_kernel(w_ref, grad_ref, out_ref):
    count, _, width = out_ref.shape
    for j in range(count):
        out_ref[j] = lax.dot_general(
            w_ref[...],
            grad_ref[j * width : (j + 1) * width, :],
            (((1,), (1,)), ((), ())),
            preferred_element_type=jnp.float32,
        )


def sigmoid(value):
    return 0.5 + 0.5 * jnp.tanh(0.5 * value)


def slot_value(end, refs, slot):
    if slot == 0:
        return refs[0][...].astype(jnp.float32)
    if slot == 1:
        return refs[1][...].astype(jnp.float32)
    at_end, at_middle = refs[2:4] if slot == 2 else refs[4:6]
    return jnp.where(end, at_end[...], at_middle[...]).astype(jnp.float32)


def place(k_ref, slot):
    return k_ref[0] ^ slot


def columns(index, width):
    return pl.ds(pl.multiple_of(index * width, width), width)


def down_kernel(factors, k_ref, *refs):
    gates, uppers = refs[:6], refs[6:12]
    grad_ref, hidden = refs[12], refs[-1]
    out_ref = refs[-4] if factors else refs[-2]
    width = gates[0].shape[1]
    end = k_ref[1] == 1
    for slot in range(4):
        gate, upper = slot_value(end, gates, slot), slot_value(end, uppers, slot)
        j = place(k_ref, slot)
        sigma = sigmoid(gate)
        active = gate * sigma
        hidden[:, columns(j, width)] = (active * upper).astype(jnp.bfloat16)
        if factors:
            refs[-3][j] = active
            refs[-2][j] = upper * sigma * (1.0 + gate * (1.0 - sigma))
    features = grad_ref.shape[1]
    step = min(features, 512)
    for c in range(0, features, step):
        cols = slice(c, c + step)
        out_ref[:, cols] = jnp.dot(
            hidden[...], grad_ref[:, cols], preferred_element_type=jnp.float32
        ).astype(jnp.bfloat16)


def main_kernel(has_acc, k_ref, *refs):
    gates, uppers = refs[:6], refs[6:12]
    part, r1, r2, r3, x_hbm, wg_ref, wu_ref = refs[12:19]
    acc_in = refs[19] if has_acc else None
    acc_out, gate_out, up_out = refs[-11:-8]
    gate_grad, up_grad, gate_turned, up_turned, x_ref, acc, sems, out_sems = refs[-8:]
    block, width = gates[0].shape
    end = k_ref[1] == 1
    first = pl.program_id(0) == 0
    x_copy = pltpu.make_async_copy(x_hbm, x_ref, sems.at[0])
    acc_copy = pltpu.make_async_copy(acc_in, acc, sems.at[1]) if has_acc else None

    @pl.when(first)
    def _():
        x_copy.start()
        if has_acc:
            acc_copy.start()
        else:
            acc[...] = jnp.zeros_like(acc)

    for slot in range(4):
        gate, upper = slot_value(end, gates, slot), slot_value(end, uppers, slot)
        j = place(k_ref, slot)
        at = columns(j, width)
        hidden_grad = (
            part[j]
            + r2[j].astype(jnp.float32)
            + jnp.where(end, r3[j], r1[j]).astype(jnp.float32)
        )
        sigma = sigmoid(gate)
        up_value = (hidden_grad * (gate * sigma)).astype(jnp.bfloat16)
        gate_value = (
            hidden_grad * upper * sigma * (1.0 + gate * (1.0 - sigma))
        ).astype(jnp.bfloat16)
        up_grad[:, at] = up_value
        gate_grad[:, at] = gate_value
        up_turned[at, :] = up_value.T
        gate_turned[at, :] = gate_value.T

    features = x_ref.shape[1]
    step = min(features, 512)
    tiles = [slice(c, c + step) for c in range(0, features, step)]

    @pl.when(first)
    def _():
        x_copy.wait()

    for cols in tiles:
        gate_out[:, cols] = jnp.dot(
            gate_grad[...], x_ref[:, cols], preferred_element_type=jnp.float32
        ).astype(jnp.bfloat16)

    if has_acc:

        @pl.when(first)
        def _():
            acc_copy.wait()

    last = pl.program_id(0) == pl.num_programs(0) - 1
    out_copies = [
        pltpu.make_async_copy(acc.at[:, cols], acc_out.at[:, cols], out_sems.at[i])
        for i, cols in enumerate(tiles)
    ]
    for i, cols in enumerate(tiles):
        acc[:, cols] += jnp.dot(
            gate_turned[...], wg_ref[:, cols], preferred_element_type=jnp.float32
        ) + jnp.dot(
            up_turned[...], wu_ref[:, cols], preferred_element_type=jnp.float32
        )
        pl.when(last)(out_copies[i].start)

    for cols in tiles:
        up_out[:, cols] = jnp.dot(
            up_grad[...], x_ref[:, cols], preferred_element_type=jnp.float32
        ).astype(jnp.bfloat16)

    @pl.when(last)
    def _():
        for copy in out_copies:
            copy.wait()


def token_kernel(rows, *refs):
    up_factor, gate_factor, part, r1, r2, r3, wg_ref, wu_ref, acc_in = refs[1:10]
    k_ref, (gate_out, up_out, acc, rounded, gate_grad, up_grad) = refs[0], refs[10:]
    count, size, width = part.shape
    ragged = rows < size
    end = k_ref[1] == 1

    def valid(value):
        if not ragged:
            return value
        at = lax.broadcasted_iota(jnp.int32, value.shape, 0)
        return jnp.where(at < rows, value, jnp.zeros_like(value))

    @pl.when(pl.program_id(0) == 0)
    def _():
        for j in range(count):
            hidden_grad = (
                part[j]
                + r2[j].astype(jnp.float32)
                + jnp.where(end, r3[j], r1[j]).astype(jnp.float32)
            )
            up_value = valid((hidden_grad * up_factor[j]).astype(jnp.bfloat16))
            gate_value = valid((hidden_grad * gate_factor[j]).astype(jnp.bfloat16))
            up_out[j] = up_value
            gate_out[j] = gate_value
            up_grad[j * width : (j + 1) * width, :] = up_value.T
            gate_grad[j * width : (j + 1) * width, :] = gate_value.T

    more = jnp.dot(
        gate_grad[...], valid(wg_ref[...]), preferred_element_type=jnp.float32
    ) + jnp.dot(up_grad[...], valid(wu_ref[...]), preferred_element_type=jnp.float32)
    value = acc_in[...] + more.reshape(acc.shape)
    acc[...] = value
    rounded[...] = value.astype(jnp.bfloat16)


def weight_kernel(parts, *refs):
    x_ref, out_ref, grad = refs[parts], refs[-2], refs[-1]
    count, _, width = refs[0].shape
    for q in range(parts):
        for j in range(count):
            at = (j * parts + q) * width
            grad[:, at : at + width] = refs[q][j]
    features = x_ref.shape[1]
    step = min(features, 512)
    for c in range(0, features, step):
        cols = slice(c, c + step)
        out_ref[:, cols] = jnp.dot(
            grad[...], x_ref[:, cols], preferred_element_type=jnp.float32
        ).astype(jnp.bfloat16)


def once(shape):
    return pl.BlockSpec(shape, lambda i, *k: (0, 0), pipeline_mode=pl.Buffered(1))


def sum_group(w_down, grad_whole, a, size, count):
    tokens, features = grad_whole.shape
    block = block_rows(size)
    blocks = size // block
    width = tokens // count
    return pl.pallas_call(
        sum_kernel,
        grid=(blocks,),
        in_specs=[
            pl.BlockSpec((block, features), lambda i: (a * blocks + i, 0)),
            once((tokens, features)),
        ],
        out_specs=pl.BlockSpec((count, block, width), lambda i: (0, i, 0)),
        out_shape=jax.ShapeDtypeStruct((count, size, width), jnp.float32),
        compiler_params=pltpu.CompilerParams(vmem_limit_bytes=VMEM_LIMIT),
        cost_estimate=pl.CostEstimate(
            flops=2 * size * tokens * features,
            bytes_accessed=size * (features * 2 + tokens * 4),
            transcendentals=0,
        ),
    )(w_down, grad_whole)


def slot_specs(a, block, width, at=0):
    gate = pl.BlockSpec((None, block, width), lambda i, k: (a % 2, at + i, 0))
    upper = pl.BlockSpec((None, block, width), lambda i, k: (2 + a % 2, at + i, 0))
    return [gate] * 6 + [upper] * 6


def down_group(k, slots, grad_whole, out, a, size, total, factors):
    tokens, features = grad_whole.shape
    width = slots[0].shape[2]
    block = block_rows(size)
    blocks = size // block
    specs = slot_specs(a, block, width) + [once((tokens, features))]
    args = list(slots) * 2 + [grad_whole]
    aliases = {}
    if out is not None:
        aliases[1 + len(args)] = 0
        args.append(out)
        specs.append(pl.BlockSpec(memory_space=pl.ANY))
    count = slots[0].shape[0]
    wide = pl.BlockSpec((count, block, width), lambda i, k: (0, i, 0))
    factor = jax.ShapeDtypeStruct((count, size, width), jnp.float32)
    return pl.pallas_call(
        functools.partial(down_kernel, factors),
        grid_spec=pltpu.PrefetchScalarGridSpec(
            num_scalar_prefetch=1,
            grid=(blocks,),
            in_specs=specs,
            out_specs=[
                pl.BlockSpec((block, features), lambda i, k: (a * blocks + i, 0))
            ]
            + [wide] * (2 * factors),
            scratch_shapes=[pltpu.VMEM((block, tokens), jnp.bfloat16)],
        ),
        out_shape=[jax.ShapeDtypeStruct((total, features), jnp.bfloat16)]
        + [factor] * (2 * factors),
        input_output_aliases=aliases,
        compiler_params=pltpu.CompilerParams(vmem_limit_bytes=VMEM_LIMIT),
        cost_estimate=pl.CostEstimate(
            flops=2 * size * tokens * features,
            bytes_accessed=size * (features * 2 + tokens * 4),
            transcendentals=size * tokens,
        ),
    )(k, *args)


def main_group(k, slots, sums, r3, x_whole, wg, wu, acc, outs, a, run, size, total):
    tokens, features = x_whole.shape
    count, _, width = slots[0].shape
    block = block_rows(size)
    base = a * (size // block) + run[0]
    blocks = run[1] - run[0]
    wide = pl.BlockSpec((count, block, width), lambda i, k: (0, run[0] + i, 0))
    weight = pl.BlockSpec((block, features), lambda i, k: (base + i, 0))
    specs = (
        slot_specs(a, block, width, run[0])
        + [wide] * 3
        + [pl.BlockSpec((count, block, width), lambda i, k: (0, i, 0))]
        + [pl.BlockSpec(memory_space=pl.ANY), weight, weight]
    )
    args = list(slots) * 2 + list(sums) + [r3, x_whole, wg, wu]
    aliases = {}
    if acc is not None:
        aliases[1 + len(args)] = 0
        args.append(acc)
        specs.append(pl.BlockSpec(memory_space=pl.ANY))
        for i, out in enumerate(outs):
            aliases[1 + len(args)] = 1 + i
            args.append(out)
            specs.append(pl.BlockSpec(memory_space=pl.ANY))
    wgrad = jax.ShapeDtypeStruct((total, features), jnp.bfloat16)
    size = blocks * block
    return pl.pallas_call(
        functools.partial(main_kernel, acc is not None),
        grid_spec=pltpu.PrefetchScalarGridSpec(
            num_scalar_prefetch=1,
            grid=(blocks,),
            in_specs=specs,
            out_specs=(pl.BlockSpec(memory_space=pl.ANY), weight, weight),
            scratch_shapes=[pltpu.VMEM((block, tokens), jnp.bfloat16)] * 2
            + [pltpu.VMEM((tokens, block), jnp.bfloat16)] * 2
            + [
                pltpu.VMEM((tokens, features), jnp.bfloat16),
                pltpu.VMEM((tokens, features), jnp.float32),
                pltpu.SemaphoreType.DMA((2,)),
                pltpu.SemaphoreType.DMA((-(-features // min(features, 512)),)),
            ],
        ),
        out_shape=(
            jax.ShapeDtypeStruct((tokens, features), jnp.float32),
            wgrad,
            wgrad,
        ),
        input_output_aliases=aliases,
        compiler_params=pltpu.CompilerParams(vmem_limit_bytes=VMEM_LIMIT),
        cost_estimate=pl.CostEstimate(
            flops=8 * size * tokens * features,
            bytes_accessed=size * (features * 8 + tokens * 14),
            transcendentals=size * tokens,
        ),
    )(k, *args)


def token_group(k, factors, sums, r3, wg, wu, acc, q, a, size, total):
    tokens, features = acc.shape
    count, _, width = r3.shape
    step = min(features, 512)
    parts = tokens // (count * width)

    def split(value):
        return value.reshape((count, parts) + value.shape[1:])

    kept = pl.Buffered(1)
    some = pl.BlockSpec(
        (count, None, size, width), lambda i, k: (0, q, 0, 0), pipeline_mode=kept
    )
    wide = pl.BlockSpec(
        (count, size, width), lambda i, k: (0, 0, 0), pipeline_mode=kept
    )
    weight = pl.BlockSpec((size, step), lambda i, k: (a, i))
    rows = min(size, total - a * size)
    grad = jax.ShapeDtypeStruct((count, size, width), jnp.bfloat16)
    whole = pl.BlockSpec((count, width, step), lambda i, k: (0, 0, i))
    return pl.pallas_call(
        functools.partial(token_kernel, rows),
        grid_spec=pltpu.PrefetchScalarGridSpec(
            num_scalar_prefetch=1,
            grid=(-(-features // step),),
            in_specs=[some] * 5
            + [wide, weight, weight]
            + [
                pl.BlockSpec(
                    (count, None, width, step), lambda i, k: (0, q, 0, i)
                )
            ],
            out_specs=[wide, wide, whole, whole],
            scratch_shapes=[pltpu.VMEM((count * width, size), jnp.bfloat16)] * 2,
        ),
        out_shape=[
            grad,
            grad,
            jax.ShapeDtypeStruct((count, width, features), jnp.float32),
            jax.ShapeDtypeStruct((count, width, features), jnp.bfloat16),
        ],
        compiler_params=pltpu.CompilerParams(vmem_limit_bytes=VMEM_LIMIT),
        cost_estimate=pl.CostEstimate(
            flops=4 * size * count * width * features,
            bytes_accessed=size * (features * 4 + count * width * 22),
            transcendentals=0,
        ),
    )(
        k,
        *[split(f) for f in factors],
        *[split(s) for s in sums],
        r3,
        wg,
        wu,
        acc.reshape(count, parts, width, features),
    )


def weight_group(grads, x_whole, out, a, size, after):
    tokens, features = x_whole.shape
    count, _, width = grads[0].shape
    block = block_rows(size)
    blocks = size // block
    wide = pl.BlockSpec((count, block, width), lambda i: (0, i, 0))
    return pl.pallas_call(
        functools.partial(weight_kernel, len(grads)),
        grid=(blocks,),
        in_specs=[wide] * len(grads)
        + [once((tokens, features)), pl.BlockSpec(memory_space=pl.ANY)]
        + [pl.BlockSpec(memory_space=pl.ANY)] * len(after),
        out_specs=pl.BlockSpec((block, features), lambda i: (a * blocks + i, 0)),
        scratch_shapes=[pltpu.VMEM((block, tokens), jnp.bfloat16)],
        out_shape=jax.ShapeDtypeStruct(out.shape, out.dtype),
        input_output_aliases={len(grads) + 1: 0},
        compiler_params=pltpu.CompilerParams(vmem_limit_bytes=VMEM_LIMIT),
        cost_estimate=pl.CostEstimate(
            flops=2 * size * tokens * features,
            bytes_accessed=size * (features * 2 + tokens * 2),
            transcendentals=0,
        ),
    )(*grads, x_whole, out, *after)


def total_of(terms):
    return functools.reduce(jnp.add, [t.astype(jnp.float32) for t in terms])


def halve(terms, axis, mine, pairs):
    shape = terms[0].shape
    size = shape[axis]
    rest = shape[:axis] + (size // 2,) + shape[axis + 1 :]

    def pick(value, which):
        view = value.reshape(shape[:axis] + (size // 2, 2) + shape[axis + 1 :])
        part = lax.dynamic_index_in_dim(view, which, axis + 1, keepdims=False)
        return part.reshape(rest)

    away = total_of([pick(t, 1 - mine) for t in terms]).astype(jnp.bfloat16)
    got = lax.ppermute(away, ("wt", "dep"), pairs)
    return [pick(t, mine) for t in terms] + [got]


def scatter_plan(q, n_wt, n_dep):
    at_wt, at_dep = lax.axis_index("wt"), lax.axis_index("dep")

    def pairs(bit_wt, bit_dep):
        return [
            (w * n_dep + d, (w ^ bit_wt) * n_dep + (d ^ bit_dep))
            for w in range(n_wt)
            for d in range(n_dep)
            if w % 2 == q
        ]

    inward = [
        (w * n_dep + d, (w ^ 1) * n_dep + d)
        for w in range(n_wt)
        for d in range(n_dep)
        if w % 2 != q
    ]
    over_wt, over_dep = [], []
    bit = 2
    while bit < n_wt:
        over_wt.append((0, (at_wt // bit) % 2, pairs(bit, 0)))
        bit *= 2
    bit = 1
    while bit < n_dep:
        over_dep.append((1, (at_dep // bit) % 2, pairs(0, bit)))
        bit *= 2
    return inward, over_wt + over_dep if q == 0 else over_dep + over_wt


def own_half(gate, upper, half, size):
    first, last = 2 * half * size, 2 * (half + 1) * size
    parts = []
    for whole in (gate, upper):
        part = whole[first : min(last, whole.shape[0])]
        part = jnp.pad(part, ((0, last - first - part.shape[0]), (0, 0)))
        parts.append(part.reshape(2, size, -1))
    return jnp.concatenate(parts, axis=0)


def per_device(n_wt, n_dep, x_saved, out_grad, gate_pre, up_pre, w_gate, w_up, w_down):
    index = lax.axis_index("inp")
    end = (index == 0) | (index == 3)
    k = jnp.stack([index, end]).astype(jnp.int32)
    total = w_down.shape[0]
    size = 16 * -(-total // (16 * GROUPS))
    gate, upper = gate_pre.T, up_pre.T
    wg, wu = w_gate.T, w_up.T

    def rounded(part, got):
        return (part + got.astype(jnp.float32)).astype(jnp.bfloat16)

    own = [own_half(gate, upper, half, size) for half in range(2)]
    swap, middle = [], []
    for step in range(2):
        swap.append(send(own[step], SWAP))
        middle.append(send(own[step], MIDDLE))
    x_whole, grad_whole = (
        lax.all_gather(x_saved, ("wt", "dep"), axis=0, tiled=True),
        lax.all_gather(out_grad, ("wt", "dep"), axis=0, tiled=True),
    )
    part = [sum_group(w_down, grad_whole, a, size, 4) for a in range(GROUPS)]
    down = None
    acc, wgrads = None, (None, None)
    last = GROUPS - 1
    factors = None

    def slots_of(a):
        h = a // 2
        return [own[h], swap[h], swap[2 + h], middle[2 + h], swap[4 + h], middle[h]]

    for step in range(2, 8):
        if step < 4:
            swap[step - 2] = tie(swap[step - 2], part[step - 2])
            middle.append(send(swap[step - 2], MIDDLE))
        if step < 6:
            outward = part[step - 2].astype(jnp.bfloat16)
            payload = jnp.where(end, outward, middle[step - 2])
            swap.append(send(payload, SWAP))
        else:
            swap.append(send(rounded(part[step - 6], middle[step - 2]), TO_ENDS))
        if 4 <= step:
            if step == 7:
                swap[5] = tie(swap[5], down)
            middle.append(send(rounded(part[step - 4], swap[step - 2]), MIDDLE))
        if 6 <= step:
            for a in (2 * step - 12, 2 * step - 11):
                down, *factors = down_group(
                    k, slots_of(a), grad_whole, down, a, size, total, a == last
                )

    blocks = size // block_rows(size)

    def main(a, acc, wgrads):
        sums = [part[a], swap[2 + a], middle[4 + a]]
        args = (k, slots_of(a), sums, swap[6 + a], x_whole, wg, wu, acc, wgrads)
        acc, *wgrads = main_group(*args, a, (0, blocks), size, total)
        return acc, wgrads

    def pieces(value):
        return value.reshape((2, 2) + value.shape[1:])

    middle[6] = tie(middle[6], down)
    swap.append(send(rounded(part[2], middle[6]), TO_ENDS))
    acc, wgrads = main(0, acc, wgrads)
    middle[7] = tie(middle[7], acc)
    final = []
    for q in range(2):
        payload = rounded(pieces(part[last])[:, q], pieces(middle[7])[:, q])
        if q == 1:
            acc, wgrads = main(1, acc, wgrads)
            payload = tie(payload, acc)
        final.append(send(payload, TO_ENDS))
    acc, wgrads = main(2, acc, wgrads)
    sums = [part[last], swap[2 + last], middle[4 + last]]
    gate_grads, up_grads, terms, plans = [], [], [], []
    for q in range(2):
        gate_part, up_part, value, small = token_group(
            k, factors, sums, final[q], wg, wu, acc, q, last, size, total
        )
        gate_grads.append(gate_part)
        up_grads.append(up_part)
        inward, plan = scatter_plan(q, n_wt, n_dep)
        view = (n_wt // 2, n_dep, -1, value.shape[-1])
        got = lax.ppermute(small, ("wt", "dep"), inward)
        terms.append([value.reshape(view), got.reshape(view)])
        plans.append(plan)

    def newest():
        return [t[-1] for t in terms]

    gate_wgrad = weight_group(gate_grads, x_whole, wgrads[0], last, size, newest())
    for stage in range(len(plans[0])):
        terms = [halve(t, *plan[stage]) for t, plan in zip(terms, plans)]
        if stage == 0:
            for t in terms:
                t[-1] = tie(t[-1], gate_wgrad)
            up_wgrad = weight_group(up_grads, x_whole, wgrads[1], last, size, newest())
    shares = [[t[0, 0] for t in of] for of in terms]
    even = lax.axis_index("wt") % 2 == 0
    share = [jnp.where(even, *pair) for pair in zip(*shares)]
    return (total_of(share).astype(jnp.bfloat16), gate_wgrad.T, up_wgrad.T, down)


def solution(mesh):
    placed = (
        P(("wt", "dep"), "inp"),
        P(("wt", "dep"), "inp"),
        P("inp", ("wt", "dep")),
        P("inp", ("wt", "dep")),
        P("inp", ("wt", "dep")),
        P("inp", ("wt", "dep")),
        P(("wt", "dep"), "inp"),
    )
    return jax.shard_map(
        functools.partial(per_device, mesh.shape["wt"], mesh.shape["dep"]),
        mesh=mesh,
        in_specs=placed,
        out_specs=(
            P(("wt", "dep"), "inp"),
            P("inp", ("wt", "dep")),
            P("inp", ("wt", "dep")),
            P(("wt", "dep"), "inp"),
        ),
        check_vma=False,
    )
```

```python
import functools

import jax
import jax.numpy as jnp
from jax import lax
from jax.experimental import pallas as pl
from jax.experimental.pallas import tpu as pltpu
from jax.sharding import PartitionSpec as P

GROUPS = 4
VMEM_LIMIT = 63 * 1024 * 1024

SWAP = [(0, 1), (1, 0), (2, 3), (3, 2)]
MIDDLE = [(1, 2), (2, 1)]
TO_ENDS = [(1, 0), (2, 3)]


def tie(value, *after):
    return pl.pallas_call(
        lambda *refs: None,
        in_specs=[pl.BlockSpec(memory_space=pl.ANY)] * (1 + len(after)),
        out_specs=pl.BlockSpec(memory_space=pl.ANY),
        out_shape=jax.ShapeDtypeStruct(value.shape, value.dtype),
        input_output_aliases={0: 0},
    )(value, *after)


def send(value, pairs):
    return lax.ppermute(value, "inp", pairs)


def block_rows(rows):
    units = rows // 16
    return 16 * max(n for n in range(1, 33) if units % n == 0)


def sum_kernel(w_ref, grad_ref, out_ref):
    count, _, width = out_ref.shape
    for j in range(count):
        out_ref[j] = lax.dot_general(
            w_ref[...],
            grad_ref[j * width : (j + 1) * width, :],
            (((1,), (1,)), ((), ())),
            preferred_element_type=jnp.float32,
        )


def sigmoid(value):
    return 0.5 + 0.5 * jnp.tanh(0.5 * value)


def slot_value(end, refs, slot):
    if slot == 0:
        return refs[0][...].astype(jnp.float32)
    if slot == 1:
        return refs[1][...].astype(jnp.float32)
    at_end, at_middle = refs[2:4] if slot == 2 else refs[4:6]
    return jnp.where(end, at_end[...], at_middle[...]).astype(jnp.float32)


def place(k_ref, slot):
    return k_ref[0] ^ slot


def columns(index, width):
    return pl.ds(pl.multiple_of(index * width, width), width)


def down_kernel(factors, k_ref, *refs):
    gates, uppers = refs[:6], refs[6:12]
    grad_ref, hidden = refs[12], refs[-1]
    out_ref = refs[-4] if factors else refs[-2]
    width = gates[0].shape[1]
    end = k_ref[1] == 1
    for slot in range(4):
        gate, upper = slot_value(end, gates, slot), slot_value(end, uppers, slot)
        j = place(k_ref, slot)
        sigma = sigmoid(gate)
        active = gate * sigma
        hidden[:, columns(j, width)] = (active * upper).astype(jnp.bfloat16)
        if factors:
            refs[-3][j] = active
            refs[-2][j] = upper * sigma * (1.0 + gate * (1.0 - sigma))
    features = grad_ref.shape[1]
    step = min(features, 512)
    for c in range(0, features, step):
        cols = slice(c, c + step)
        out_ref[:, cols] = jnp.dot(
            hidden[...], grad_ref[:, cols], preferred_element_type=jnp.float32
        ).astype(jnp.bfloat16)


def main_kernel(has_acc, k_ref, *refs):
    gates, uppers = refs[:6], refs[6:12]
    part, r1, r2, r3, x_ref, wg_ref, wu_ref = refs[12:19]
    acc, gate_out, up_out, gate_grad, up_grad, gate_turned, up_turned = refs[-7:]
    width = gates[0].shape[1]
    end = k_ref[1] == 1

    @pl.when(pl.program_id(0) == 0)
    def _():
        for slot in range(4):
            gate, upper = slot_value(end, gates, slot), slot_value(end, uppers, slot)
            j = place(k_ref, slot)
            at = columns(j, width)
            hidden_grad = (
                part[j]
                + r2[j].astype(jnp.float32)
                + jnp.where(end, r3[j], r1[j]).astype(jnp.float32)
            )
            sigma = sigmoid(gate)
            up_value = (hidden_grad * (gate * sigma)).astype(jnp.bfloat16)
            gate_value = (
                hidden_grad * upper * sigma * (1.0 + gate * (1.0 - sigma))
            ).astype(jnp.bfloat16)
            up_grad[:, at] = up_value
            gate_grad[:, at] = gate_value
            up_turned[at, :] = up_value.T
            gate_turned[at, :] = gate_value.T

    gate_out[...] = jnp.dot(
        gate_grad[...], x_ref[...], preferred_element_type=jnp.float32
    ).astype(jnp.bfloat16)
    up_out[...] = jnp.dot(
        up_grad[...], x_ref[...], preferred_element_type=jnp.float32
    ).astype(jnp.bfloat16)
    more = jnp.dot(
        gate_turned[...], wg_ref[...], preferred_element_type=jnp.float32
    ) + jnp.dot(up_turned[...], wu_ref[...], preferred_element_type=jnp.float32)
    acc[...] = refs[19][...] + more if has_acc else more


def token_kernel(rows, *refs):
    up_factor, gate_factor, part, r1, r2, r3, wg_ref, wu_ref, acc_in = refs[1:10]
    k_ref, (gate_out, up_out, acc, rounded, gate_grad, up_grad) = refs[0], refs[10:]
    count, size, width = part.shape
    ragged = rows < size
    end = k_ref[1] == 1

    def valid(value):
        if not ragged:
            return value
        at = lax.broadcasted_iota(jnp.int32, value.shape, 0)
        return jnp.where(at < rows, value, jnp.zeros_like(value))

    @pl.when(pl.program_id(0) == 0)
    def _():
        for j in range(count):
            hidden_grad = (
                part[j]
                + r2[j].astype(jnp.float32)
                + jnp.where(end, r3[j], r1[j]).astype(jnp.float32)
            )
            up_value = valid((hidden_grad * up_factor[j]).astype(jnp.bfloat16))
            gate_value = valid((hidden_grad * gate_factor[j]).astype(jnp.bfloat16))
            up_out[j] = up_value
            gate_out[j] = gate_value
            up_grad[j * width : (j + 1) * width, :] = up_value.T
            gate_grad[j * width : (j + 1) * width, :] = gate_value.T

    more = jnp.dot(
        gate_grad[...], valid(wg_ref[...]), preferred_element_type=jnp.float32
    ) + jnp.dot(up_grad[...], valid(wu_ref[...]), preferred_element_type=jnp.float32)
    value = acc_in[...] + more.reshape(acc.shape)
    acc[...] = value
    rounded[...] = value.astype(jnp.bfloat16)


def weight_kernel(parts, *refs):
    x_ref, out_ref, grad = refs[parts], refs[-2], refs[-1]
    count, _, width = refs[0].shape

    @pl.when(pl.program_id(0) == 0)
    def _():
        for q in range(parts):
            for j in range(count):
                at = (j * parts + q) * width
                grad[:, at : at + width] = refs[q][j]

    out_ref[...] = jnp.dot(
        grad[...], x_ref[...], preferred_element_type=jnp.float32
    ).astype(jnp.bfloat16)


def once(shape):
    return pl.BlockSpec(shape, lambda i, *k: (0, 0), pipeline_mode=pl.Buffered(1))


def sum_group(w_down, grad_whole, a, size, count):
    tokens, features = grad_whole.shape
    block = block_rows(size)
    blocks = size // block
    width = tokens // count
    return pl.pallas_call(
        sum_kernel,
        grid=(blocks,),
        in_specs=[
            pl.BlockSpec((block, features), lambda i: (a * blocks + i, 0)),
            once((tokens, features)),
        ],
        out_specs=pl.BlockSpec((count, block, width), lambda i: (0, i, 0)),
        out_shape=jax.ShapeDtypeStruct((count, size, width), jnp.float32),
        compiler_params=pltpu.CompilerParams(vmem_limit_bytes=VMEM_LIMIT),
        cost_estimate=pl.CostEstimate(
            flops=2 * size * tokens * features,
            bytes_accessed=size * (features * 2 + tokens * 4),
            transcendentals=0,
        ),
    )(w_down, grad_whole)


def slot_specs(a, block, width, at=0):
    gate = pl.BlockSpec((None, block, width), lambda i, k: (a % 2, at + i, 0))
    upper = pl.BlockSpec((None, block, width), lambda i, k: (2 + a % 2, at + i, 0))
    return [gate] * 6 + [upper] * 6


def down_group(k, slots, grad_whole, out, a, size, total, factors):
    tokens, features = grad_whole.shape
    width = slots[0].shape[2]
    block = block_rows(size)
    blocks = size // block
    specs = slot_specs(a, block, width) + [once((tokens, features))]
    args = list(slots) * 2 + [grad_whole]
    aliases = {}
    if out is not None:
        aliases[1 + len(args)] = 0
        args.append(out)
        specs.append(pl.BlockSpec(memory_space=pl.ANY))
    count = slots[0].shape[0]
    wide = pl.BlockSpec((count, block, width), lambda i, k: (0, i, 0))
    factor = jax.ShapeDtypeStruct((count, size, width), jnp.float32)
    return pl.pallas_call(
        functools.partial(down_kernel, factors),
        grid_spec=pltpu.PrefetchScalarGridSpec(
            num_scalar_prefetch=1,
            grid=(blocks,),
            in_specs=specs,
            out_specs=[
                pl.BlockSpec((block, features), lambda i, k: (a * blocks + i, 0))
            ]
            + [wide] * (2 * factors),
            scratch_shapes=[pltpu.VMEM((block, tokens), jnp.bfloat16)],
        ),
        out_shape=[jax.ShapeDtypeStruct((total, features), jnp.bfloat16)]
        + [factor] * (2 * factors),
        input_output_aliases=aliases,
        compiler_params=pltpu.CompilerParams(vmem_limit_bytes=VMEM_LIMIT),
        cost_estimate=pl.CostEstimate(
            flops=2 * size * tokens * features,
            bytes_accessed=size * (features * 2 + tokens * 4),
            transcendentals=size * tokens,
        ),
    )(k, *args)


def main_group(k, slots, sums, x_whole, wg, wu, acc, outs, a, size, total):
    tokens, features = x_whole.shape
    count, _, width = slots[0].shape
    step = min(features, 512)
    kept = pl.Buffered(1)
    gate = pl.BlockSpec(
        (None, size, width), lambda i, k: (a % 2, 0, 0), pipeline_mode=kept
    )
    upper = pl.BlockSpec(
        (None, size, width), lambda i, k: (2 + a % 2, 0, 0), pipeline_mode=kept
    )
    wide = pl.BlockSpec(
        (count, size, width), lambda i, k: (0, 0, 0), pipeline_mode=kept
    )
    weight = pl.BlockSpec((size, step), lambda i, k: (a, i))
    tile = pl.BlockSpec((tokens, step), lambda i, k: (0, i))
    specs = [gate] * 6 + [upper] * 6 + [wide] * 4 + [tile, weight, weight]
    args = list(slots) * 2 + list(sums) + [x_whole, wg, wu]
    aliases = {}
    if acc is not None:
        aliases[1 + len(args)] = 0
        args.append(acc)
        specs.append(tile)
        for i, out in enumerate(outs):
            aliases[1 + len(args)] = 1 + i
            args.append(out)
            specs.append(pl.BlockSpec(memory_space=pl.ANY))
    wgrad = jax.ShapeDtypeStruct((total, features), jnp.bfloat16)
    return pl.pallas_call(
        functools.partial(main_kernel, acc is not None),
        grid_spec=pltpu.PrefetchScalarGridSpec(
            num_scalar_prefetch=1,
            grid=(-(-features // step),),
            in_specs=specs,
            out_specs=(tile, weight, weight),
            scratch_shapes=[pltpu.VMEM((size, tokens), jnp.bfloat16)] * 2
            + [pltpu.VMEM((tokens, size), jnp.bfloat16)] * 2,
        ),
        out_shape=(
            jax.ShapeDtypeStruct((tokens, features), jnp.float32),
            wgrad,
            wgrad,
        ),
        input_output_aliases=aliases,
        compiler_params=pltpu.CompilerParams(vmem_limit_bytes=VMEM_LIMIT),
        cost_estimate=pl.CostEstimate(
            flops=8 * size * tokens * features,
            bytes_accessed=size * (features * 8 + tokens * 14),
            transcendentals=size * tokens,
        ),
    )(k, *args)


def token_group(k, factors, sums, r3, wg, wu, acc, q, a, size, total):
    tokens, features = acc.shape
    count, _, width = r3.shape
    step = min(features, 512)
    parts = tokens // (count * width)

    def split(value):
        return value.reshape((count, parts) + value.shape[1:])

    kept = pl.Buffered(1)
    some = pl.BlockSpec(
        (count, None, size, width), lambda i, k: (0, q, 0, 0), pipeline_mode=kept
    )
    wide = pl.BlockSpec(
        (count, size, width), lambda i, k: (0, 0, 0), pipeline_mode=kept
    )
    weight = pl.BlockSpec((size, step), lambda i, k: (a, i))
    rows = min(size, total - a * size)
    grad = jax.ShapeDtypeStruct((count, size, width), jnp.bfloat16)
    whole = pl.BlockSpec((count, width, step), lambda i, k: (0, 0, i))
    return pl.pallas_call(
        functools.partial(token_kernel, rows),
        grid_spec=pltpu.PrefetchScalarGridSpec(
            num_scalar_prefetch=1,
            grid=(-(-features // step),),
            in_specs=[some] * 5
            + [wide, weight, weight]
            + [
                pl.BlockSpec(
                    (count, None, width, step), lambda i, k: (0, q, 0, i)
                )
            ],
            out_specs=[wide, wide, whole, whole],
            scratch_shapes=[pltpu.VMEM((count * width, size), jnp.bfloat16)] * 2,
        ),
        out_shape=[
            grad,
            grad,
            jax.ShapeDtypeStruct((count, width, features), jnp.float32),
            jax.ShapeDtypeStruct((count, width, features), jnp.bfloat16),
        ],
        compiler_params=pltpu.CompilerParams(vmem_limit_bytes=VMEM_LIMIT),
        cost_estimate=pl.CostEstimate(
            flops=4 * size * count * width * features,
            bytes_accessed=size * (features * 4 + count * width * 22),
            transcendentals=0,
        ),
    )(
        k,
        *[split(f) for f in factors],
        *[split(s) for s in sums],
        r3,
        wg,
        wu,
        acc.reshape(count, parts, width, features),
    )


def weight_group(grads, x_whole, out, a, size, after):
    tokens, features = x_whole.shape
    count, _, width = grads[0].shape
    step = min(features, 512)
    wide = pl.BlockSpec(
        (count, size, width), lambda i: (0, 0, 0), pipeline_mode=pl.Buffered(1)
    )
    return pl.pallas_call(
        functools.partial(weight_kernel, len(grads)),
        grid=(-(-features // step),),
        in_specs=[wide] * len(grads)
        + [
            pl.BlockSpec((tokens, step), lambda i: (0, i)),
            pl.BlockSpec(memory_space=pl.ANY),
        ]
        + [pl.BlockSpec(memory_space=pl.ANY)] * len(after),
        out_specs=pl.BlockSpec((size, step), lambda i: (a, i)),
        scratch_shapes=[pltpu.VMEM((size, tokens), jnp.bfloat16)],
        out_shape=jax.ShapeDtypeStruct(out.shape, out.dtype),
        input_output_aliases={len(grads) + 1: 0},
        compiler_params=pltpu.CompilerParams(vmem_limit_bytes=VMEM_LIMIT),
        cost_estimate=pl.CostEstimate(
            flops=2 * size * tokens * features,
            bytes_accessed=size * (features * 2 + tokens * 2),
            transcendentals=0,
        ),
    )(*grads, x_whole, out, *after)


def total_of(terms):
    return functools.reduce(jnp.add, [t.astype(jnp.float32) for t in terms])


def halve(terms, axis, mine, pairs):
    shape = terms[0].shape
    size = shape[axis]
    rest = shape[:axis] + (size // 2,) + shape[axis + 1 :]

    def pick(value, which):
        view = value.reshape(shape[:axis] + (size // 2, 2) + shape[axis + 1 :])
        part = lax.dynamic_index_in_dim(view, which, axis + 1, keepdims=False)
        return part.reshape(rest)

    away = total_of([pick(t, 1 - mine) for t in terms]).astype(jnp.bfloat16)
    got = lax.ppermute(away, ("wt", "dep"), pairs)
    return [pick(t, mine) for t in terms] + [got]


def scatter_plan(q, n_wt, n_dep):
    at_wt, at_dep = lax.axis_index("wt"), lax.axis_index("dep")

    def pairs(bit_wt, bit_dep):
        return [
            (w * n_dep + d, (w ^ bit_wt) * n_dep + (d ^ bit_dep))
            for w in range(n_wt)
            for d in range(n_dep)
            if w % 2 == q
        ]

    inward = [
        (w * n_dep + d, (w ^ 1) * n_dep + d)
        for w in range(n_wt)
        for d in range(n_dep)
        if w % 2 != q
    ]
    over_wt, over_dep = [], []
    bit = 2
    while bit < n_wt:
        over_wt.append((0, (at_wt // bit) % 2, pairs(bit, 0)))
        bit *= 2
    bit = 1
    while bit < n_dep:
        over_dep.append((1, (at_dep // bit) % 2, pairs(0, bit)))
        bit *= 2
    return inward, over_wt + over_dep if q == 0 else over_dep + over_wt


def own_half(gate, upper, half, size):
    first, last = 2 * half * size, 2 * (half + 1) * size
    parts = []
    for whole in (gate, upper):
        part = whole[first : min(last, whole.shape[0])]
        part = jnp.pad(part, ((0, last - first - part.shape[0]), (0, 0)))
        parts.append(part.reshape(2, size, -1))
    return jnp.concatenate(parts, axis=0)


def per_device(n_wt, n_dep, x_saved, out_grad, gate_pre, up_pre, w_gate, w_up, w_down):
    index = lax.axis_index("inp")
    end = (index == 0) | (index == 3)
    k = jnp.stack([index, end]).astype(jnp.int32)
    total = w_down.shape[0]
    size = 16 * -(-total // (16 * GROUPS))
    gate, upper = gate_pre.T, up_pre.T
    wg, wu = w_gate.T, w_up.T

    def rounded(part, got):
        return (part + got.astype(jnp.float32)).astype(jnp.bfloat16)

    own = [own_half(gate, upper, half, size) for half in range(2)]
    swap, middle = [], []
    for step in range(2):
        swap.append(send(own[step], SWAP))
        middle.append(send(own[step], MIDDLE))
    x_whole, grad_whole = (
        lax.all_gather(x_saved, ("wt", "dep"), axis=0, tiled=True),
        lax.all_gather(out_grad, ("wt", "dep"), axis=0, tiled=True),
    )
    part = [sum_group(w_down, grad_whole, a, size, 4) for a in range(GROUPS)]
    down = None
    acc, wgrads = None, (None, None)
    last = GROUPS - 1
    factors = None

    def slots_of(a):
        h = a // 2
        return [own[h], swap[h], swap[2 + h], middle[2 + h], swap[4 + h], middle[h]]

    for step in range(2, 8):
        if step < 4:
            swap[step - 2] = tie(swap[step - 2], part[step - 2])
            middle.append(send(swap[step - 2], MIDDLE))
        if step < 6:
            outward = part[step - 2].astype(jnp.bfloat16)
            payload = jnp.where(end, outward, middle[step - 2])
            swap.append(send(payload, SWAP))
        else:
            swap.append(send(rounded(part[step - 6], middle[step - 2]), TO_ENDS))
        if 4 <= step:
            if step == 7:
                swap[5] = tie(swap[5], down)
            middle.append(send(rounded(part[step - 4], swap[step - 2]), MIDDLE))
        if 6 <= step:
            for a in (2 * step - 12, 2 * step - 11):
                down, *factors = down_group(
                    k, slots_of(a), grad_whole, down, a, size, total, a == last
                )

    def main(a, acc, wgrads):
        sums = [part[a], swap[2 + a], middle[4 + a], swap[6 + a]]
        args = (k, slots_of(a), sums, x_whole, wg, wu, acc, wgrads)
        acc, *wgrads = main_group(*args, a, size, total)
        return acc, wgrads

    def pieces(value):
        return value.reshape((2, 2) + value.shape[1:])

    middle[6] = tie(middle[6], down)
    swap.append(send(rounded(part[2], middle[6]), TO_ENDS))
    acc, wgrads = main(0, acc, wgrads)
    middle[7] = tie(middle[7], acc)
    final = []
    for q in range(2):
        payload = rounded(pieces(part[last])[:, q], pieces(middle[7])[:, q])
        if q == 1:
            acc, wgrads = main(1, acc, wgrads)
            payload = tie(payload, acc)
        final.append(send(payload, TO_ENDS))
    acc, wgrads = main(2, acc, wgrads)
    sums = [part[last], swap[2 + last], middle[4 + last]]
    gate_grads, up_grads, terms, plans = [], [], [], []
    for q in range(2):
        gate_part, up_part, value, small = token_group(
            k, factors, sums, final[q], wg, wu, acc, q, last, size, total
        )
        gate_grads.append(gate_part)
        up_grads.append(up_part)
        inward, plan = scatter_plan(q, n_wt, n_dep)
        view = (n_wt // 2, n_dep, -1, value.shape[-1])
        got = lax.ppermute(small, ("wt", "dep"), inward)
        terms.append([value.reshape(view), got.reshape(view)])
        plans.append(plan)

    def newest():
        return [t[-1] for t in terms]

    gate_wgrad = weight_group(gate_grads, x_whole, wgrads[0], last, size, newest())
    for stage in range(len(plans[0])):
        terms = [halve(t, *plan[stage]) for t, plan in zip(terms, plans)]
        if stage == 0:
            for t in terms:
                t[-1] = tie(t[-1], gate_wgrad)
            up_wgrad = weight_group(up_grads, x_whole, wgrads[1], last, size, newest())
    shares = [[t[0, 0] for t in of] for of in terms]
    even = lax.axis_index("wt") % 2 == 0
    share = [jnp.where(even, *pair) for pair in zip(*shares)]
    return (total_of(share).astype(jnp.bfloat16), gate_wgrad.T, up_wgrad.T, down)


def solution(mesh):
    placed = (
        P(("wt", "dep"), "inp"),
        P(("wt", "dep"), "inp"),
        P("inp", ("wt", "dep")),
        P("inp", ("wt", "dep")),
        P("inp", ("wt", "dep")),
        P("inp", ("wt", "dep")),
        P(("wt", "dep"), "inp"),
    )
    return jax.shard_map(
        functools.partial(per_device, mesh.shape["wt"], mesh.shape["dep"]),
        mesh=mesh,
        in_specs=placed,
        out_specs=(
            P(("wt", "dep"), "inp"),
            P("inp", ("wt", "dep")),
            P("inp", ("wt", "dep")),
            P(("wt", "dep"), "inp"),
        ),
        check_vma=False,
    )
```

```python
import functools

import jax
import jax.numpy as jnp
from jax import lax
from jax.experimental import pallas as pl
from jax.experimental.pallas import tpu as pltpu
from jax.sharding import PartitionSpec as P

GROUPS = 4
VMEM_LIMIT = 63 * 1024 * 1024

SWAP = [(0, 1), (1, 0), (2, 3), (3, 2)]
MIDDLE = [(1, 2), (2, 1)]
TO_ENDS = [(1, 0), (2, 3)]


def tie(value, *after):
    return pl.pallas_call(
        lambda *refs: None,
        in_specs=[pl.BlockSpec(memory_space=pl.ANY)] * (1 + len(after)),
        out_specs=pl.BlockSpec(memory_space=pl.ANY),
        out_shape=jax.ShapeDtypeStruct(value.shape, value.dtype),
        input_output_aliases={0: 0},
    )(value, *after)


def send(value, pairs):
    return lax.ppermute(value, "inp", pairs)


def block_rows(rows):
    units = rows // 16
    return 16 * max(n for n in range(1, 33) if units % n == 0)


def sum_kernel(w_ref, grad_ref, out_ref):
    count, _, width = out_ref.shape
    for j in range(count):
        out_ref[j] = lax.dot_general(
            w_ref[...],
            grad_ref[j * width : (j + 1) * width, :],
            (((1,), (1,)), ((), ())),
            preferred_element_type=jnp.float32,
        )


def sigmoid(value):
    return 0.5 + 0.5 * jnp.tanh(0.5 * value)


def slot_value(end, refs, slot):
    if slot == 0:
        return refs[0][...].astype(jnp.float32)
    if slot == 1:
        return refs[1][...].astype(jnp.float32)
    at_end, at_middle = refs[2:4] if slot == 2 else refs[4:6]
    return jnp.where(end, at_end[...], at_middle[...]).astype(jnp.float32)


def place(k_ref, slot):
    return k_ref[0] ^ slot


def columns(index, width):
    return pl.ds(pl.multiple_of(index * width, width), width)


def down_kernel(factors, k_ref, *refs):
    gates, uppers = refs[:6], refs[6:12]
    grad_ref, hidden = refs[12], refs[-1]
    out_ref = refs[-4] if factors else refs[-2]
    width = gates[0].shape[1]
    end = k_ref[1] == 1
    for slot in range(4):
        gate, upper = slot_value(end, gates, slot), slot_value(end, uppers, slot)
        j = place(k_ref, slot)
        sigma = sigmoid(gate)
        active = gate * sigma
        hidden[:, columns(j, width)] = (active * upper).astype(jnp.bfloat16)
        if factors:
            refs[-3][j] = active
            refs[-2][j] = upper * sigma * (1.0 + gate * (1.0 - sigma))
    features = grad_ref.shape[1]
    step = min(features, 512)
    for c in range(0, features, step):
        cols = slice(c, c + step)
        out_ref[:, cols] = jnp.dot(
            hidden[...], grad_ref[:, cols], preferred_element_type=jnp.float32
        ).astype(jnp.bfloat16)


def main_kernel(has_acc, k_ref, *refs):
    gates, uppers = refs[:6], refs[6:12]
    part, r1, r2, r3, x_ref, wg_ref, wu_ref = refs[12:19]
    acc, gate_out, up_out, gate_grad, up_grad, gate_turned, up_turned = refs[-7:]
    width = gates[0].shape[1]
    end = k_ref[1] == 1

    @pl.when(pl.program_id(0) == 0)
    def _():
        for slot in range(4):
            gate, upper = slot_value(end, gates, slot), slot_value(end, uppers, slot)
            j = place(k_ref, slot)
            at = columns(j, width)
            hidden_grad = (
                part[j]
                + r2[j].astype(jnp.float32)
                + jnp.where(end, r3[j], r1[j]).astype(jnp.float32)
            )
            sigma = sigmoid(gate)
            up_value = (hidden_grad * (gate * sigma)).astype(jnp.bfloat16)
            gate_value = (
                hidden_grad * upper * sigma * (1.0 + gate * (1.0 - sigma))
            ).astype(jnp.bfloat16)
            up_grad[:, at] = up_value
            gate_grad[:, at] = gate_value
            up_turned[at, :] = up_value.T
            gate_turned[at, :] = gate_value.T

    gate_out[...] = jnp.dot(
        gate_grad[...], x_ref[...], preferred_element_type=jnp.float32
    ).astype(jnp.bfloat16)
    up_out[...] = jnp.dot(
        up_grad[...], x_ref[...], preferred_element_type=jnp.float32
    ).astype(jnp.bfloat16)
    more = jnp.dot(
        gate_turned[...], wg_ref[...], preferred_element_type=jnp.float32
    ) + jnp.dot(up_turned[...], wu_ref[...], preferred_element_type=jnp.float32)
    acc[...] = refs[19][...] + more if has_acc else more


def token_kernel(rows, *refs):
    up_factor, gate_factor, part, r1, r2, r3, wg_ref, wu_ref, acc_in = refs[1:10]
    k_ref, (gate_out, up_out, acc, rounded, gate_grad, up_grad) = refs[0], refs[10:]
    count, size, width = part.shape
    ragged = rows < size
    end = k_ref[1] == 1

    def valid(value):
        if not ragged:
            return value
        at = lax.broadcasted_iota(jnp.int32, value.shape, 0)
        return jnp.where(at < rows, value, jnp.zeros_like(value))

    @pl.when(pl.program_id(0) == 0)
    def _():
        for j in range(count):
            hidden_grad = (
                part[j]
                + r2[j].astype(jnp.float32)
                + jnp.where(end, r3[j], r1[j]).astype(jnp.float32)
            )
            up_value = valid((hidden_grad * up_factor[j]).astype(jnp.bfloat16))
            gate_value = valid((hidden_grad * gate_factor[j]).astype(jnp.bfloat16))
            up_out[j] = up_value
            gate_out[j] = gate_value
            up_grad[j * width : (j + 1) * width, :] = up_value.T
            gate_grad[j * width : (j + 1) * width, :] = gate_value.T

    more = jnp.dot(
        gate_grad[...], valid(wg_ref[...]), preferred_element_type=jnp.float32
    ) + jnp.dot(up_grad[...], valid(wu_ref[...]), preferred_element_type=jnp.float32)
    value = acc_in[...] + more.reshape(acc.shape)
    acc[...] = value
    rounded[...] = value.astype(jnp.bfloat16)


def weight_kernel(parts, *refs):
    x_ref, out_ref, grad = refs[parts], refs[-2], refs[-1]
    count, _, width = refs[0].shape

    @pl.when(pl.program_id(0) == 0)
    def _():
        for q in range(parts):
            for j in range(count):
                at = (j * parts + q) * width
                grad[:, at : at + width] = refs[q][j]

    out_ref[...] = jnp.dot(
        grad[...], x_ref[...], preferred_element_type=jnp.float32
    ).astype(jnp.bfloat16)


def once(shape):
    return pl.BlockSpec(shape, lambda i, *k: (0, 0), pipeline_mode=pl.Buffered(1))


def sum_group(w_down, grad_whole, a, size, count):
    tokens, features = grad_whole.shape
    block = block_rows(size)
    blocks = size // block
    width = tokens // count
    return pl.pallas_call(
        sum_kernel,
        grid=(blocks,),
        in_specs=[
            pl.BlockSpec((block, features), lambda i: (a * blocks + i, 0)),
            once((tokens, features)),
        ],
        out_specs=pl.BlockSpec((count, block, width), lambda i: (0, i, 0)),
        out_shape=jax.ShapeDtypeStruct((count, size, width), jnp.float32),
        compiler_params=pltpu.CompilerParams(vmem_limit_bytes=VMEM_LIMIT),
        cost_estimate=pl.CostEstimate(
            flops=2 * size * tokens * features,
            bytes_accessed=size * (features * 2 + tokens * 4),
            transcendentals=0,
        ),
    )(w_down, grad_whole)


def slot_specs(a, block, width, at=0):
    gate = pl.BlockSpec((None, block, width), lambda i, k: (a % 2, at + i, 0))
    upper = pl.BlockSpec((None, block, width), lambda i, k: (2 + a % 2, at + i, 0))
    return [gate] * 6 + [upper] * 6


def down_group(k, slots, grad_whole, out, a, size, total, factors):
    tokens, features = grad_whole.shape
    width = slots[0].shape[2]
    block = block_rows(size)
    blocks = size // block
    specs = slot_specs(a, block, width) + [once((tokens, features))]
    args = list(slots) * 2 + [grad_whole]
    aliases = {}
    if out is not None:
        aliases[1 + len(args)] = 0
        args.append(out)
        specs.append(pl.BlockSpec(memory_space=pl.ANY))
    count = slots[0].shape[0]
    wide = pl.BlockSpec((count, block, width), lambda i, k: (0, i, 0))
    factor = jax.ShapeDtypeStruct((count, size, width), jnp.float32)
    return pl.pallas_call(
        functools.partial(down_kernel, factors),
        grid_spec=pltpu.PrefetchScalarGridSpec(
            num_scalar_prefetch=1,
            grid=(blocks,),
            in_specs=specs,
            out_specs=[
                pl.BlockSpec((block, features), lambda i, k: (a * blocks + i, 0))
            ]
            + [wide] * (2 * factors),
            scratch_shapes=[pltpu.VMEM((block, tokens), jnp.bfloat16)],
        ),
        out_shape=[jax.ShapeDtypeStruct((total, features), jnp.bfloat16)]
        + [factor] * (2 * factors),
        input_output_aliases=aliases,
        compiler_params=pltpu.CompilerParams(vmem_limit_bytes=VMEM_LIMIT),
        cost_estimate=pl.CostEstimate(
            flops=2 * size * tokens * features,
            bytes_accessed=size * (features * 2 + tokens * 4),
            transcendentals=size * tokens,
        ),
    )(k, *args)


def main_group(k, slots, sums, x_whole, wg, wu, acc, outs, a, cut, size, total):
    tokens, features = x_whole.shape
    count, _, width = slots[0].shape
    step = min(features, 512)
    at, size = cut[0], size // cut[1]
    base = a * cut[1] + at
    kept = pl.Buffered(1)
    gate = pl.BlockSpec(
        (None, size, width), lambda i, k: (a % 2, at, 0), pipeline_mode=kept
    )
    upper = pl.BlockSpec(
        (None, size, width), lambda i, k: (2 + a % 2, at, 0), pipeline_mode=kept
    )
    wide = pl.BlockSpec(
        (count, size, width), lambda i, k: (0, at, 0), pipeline_mode=kept
    )
    alone = pl.BlockSpec(
        (count, size, width), lambda i, k: (0, 0, 0), pipeline_mode=kept
    )
    weight = pl.BlockSpec((size, step), lambda i, k: (base, i))
    tile = pl.BlockSpec((tokens, step), lambda i, k: (0, i))
    specs = [gate] * 6 + [upper] * 6 + [wide] * 3 + [alone, tile, weight, weight]
    args = list(slots) * 2 + list(sums) + [x_whole, wg, wu]
    aliases = {}
    if acc is not None:
        aliases[1 + len(args)] = 0
        args.append(acc)
        specs.append(tile)
        for i, out in enumerate(outs):
            aliases[1 + len(args)] = 1 + i
            args.append(out)
            specs.append(pl.BlockSpec(memory_space=pl.ANY))
    wgrad = jax.ShapeDtypeStruct((total, features), jnp.bfloat16)
    return pl.pallas_call(
        functools.partial(main_kernel, acc is not None),
        grid_spec=pltpu.PrefetchScalarGridSpec(
            num_scalar_prefetch=1,
            grid=(-(-features // step),),
            in_specs=specs,
            out_specs=(tile, weight, weight),
            scratch_shapes=[pltpu.VMEM((size, tokens), jnp.bfloat16)] * 2
            + [pltpu.VMEM((tokens, size), jnp.bfloat16)] * 2,
        ),
        out_shape=(
            jax.ShapeDtypeStruct((tokens, features), jnp.float32),
            wgrad,
            wgrad,
        ),
        input_output_aliases=aliases,
        compiler_params=pltpu.CompilerParams(vmem_limit_bytes=VMEM_LIMIT),
        cost_estimate=pl.CostEstimate(
            flops=8 * size * tokens * features,
            bytes_accessed=size * (features * 8 + tokens * 14),
            transcendentals=size * tokens,
        ),
    )(k, *args)


def token_group(k, factors, sums, r3, wg, wu, acc, q, a, size, total):
    tokens, features = acc.shape
    count, _, width = r3.shape
    step = min(features, 1024)
    parts = tokens // (count * width)

    def split(value):
        return value.reshape((count, parts) + value.shape[1:])

    kept = pl.Buffered(1)
    some = pl.BlockSpec(
        (count, None, size, width), lambda i, k: (0, q, 0, 0), pipeline_mode=kept
    )
    wide = pl.BlockSpec(
        (count, size, width), lambda i, k: (0, 0, 0), pipeline_mode=kept
    )
    weight = pl.BlockSpec((size, step), lambda i, k: (a, i))
    rows = min(size, total - a * size)
    grad = jax.ShapeDtypeStruct((count, size, width), jnp.bfloat16)
    whole = pl.BlockSpec((count, width, step), lambda i, k: (0, 0, i))
    return pl.pallas_call(
        functools.partial(token_kernel, rows),
        grid_spec=pltpu.PrefetchScalarGridSpec(
            num_scalar_prefetch=1,
            grid=(-(-features // step),),
            in_specs=[some] * 5
            + [wide, weight, weight]
            + [
                pl.BlockSpec(
                    (count, None, width, step), lambda i, k: (0, q, 0, i)
                )
            ],
            out_specs=[wide, wide, whole, whole],
            scratch_shapes=[pltpu.VMEM((count * width, size), jnp.bfloat16)] * 2,
        ),
        out_shape=[
            grad,
            grad,
            jax.ShapeDtypeStruct((count, width, features), jnp.float32),
            jax.ShapeDtypeStruct((count, width, features), jnp.bfloat16),
        ],
        compiler_params=pltpu.CompilerParams(vmem_limit_bytes=VMEM_LIMIT),
        cost_estimate=pl.CostEstimate(
            flops=4 * size * count * width * features,
            bytes_accessed=size * (features * 4 + count * width * 22),
            transcendentals=0,
        ),
    )(
        k,
        *[split(f) for f in factors],
        *[split(s) for s in sums],
        r3,
        wg,
        wu,
        acc.reshape(count, parts, width, features),
    )


def weight_group(grads, x_whole, out, a, size, after):
    tokens, features = x_whole.shape
    count, _, width = grads[0].shape
    step = min(features, 1024)
    wide = pl.BlockSpec(
        (count, size, width), lambda i: (0, 0, 0), pipeline_mode=pl.Buffered(1)
    )
    return pl.pallas_call(
        functools.partial(weight_kernel, len(grads)),
        grid=(-(-features // step),),
        in_specs=[wide] * len(grads)
        + [
            pl.BlockSpec((tokens, step), lambda i: (0, i)),
            pl.BlockSpec(memory_space=pl.ANY),
        ]
        + [pl.BlockSpec(memory_space=pl.ANY)] * len(after),
        out_specs=pl.BlockSpec((size, step), lambda i: (a, i)),
        scratch_shapes=[pltpu.VMEM((size, tokens), jnp.bfloat16)],
        out_shape=jax.ShapeDtypeStruct(out.shape, out.dtype),
        input_output_aliases={len(grads) + 1: 0},
        compiler_params=pltpu.CompilerParams(vmem_limit_bytes=VMEM_LIMIT),
        cost_estimate=pl.CostEstimate(
            flops=2 * size * tokens * features,
            bytes_accessed=size * (features * 2 + tokens * 2),
            transcendentals=0,
        ),
    )(*grads, x_whole, out, *after)


def total_of(terms):
    return functools.reduce(jnp.add, [t.astype(jnp.float32) for t in terms])


def halve(terms, axis, mine, pairs):
    shape = terms[0].shape
    size = shape[axis]
    rest = shape[:axis] + (size // 2,) + shape[axis + 1 :]

    def pick(value, which):
        view = value.reshape(shape[:axis] + (size // 2, 2) + shape[axis + 1 :])
        part = lax.dynamic_index_in_dim(view, which, axis + 1, keepdims=False)
        return part.reshape(rest)

    away = total_of([pick(t, 1 - mine) for t in terms]).astype(jnp.bfloat16)
    got = lax.ppermute(away, ("wt", "dep"), pairs)
    return [pick(t, mine) for t in terms] + [got]


def scatter_plan(q, n_wt, n_dep):
    at_wt, at_dep = lax.axis_index("wt"), lax.axis_index("dep")

    def pairs(bit_wt, bit_dep):
        return [
            (w * n_dep + d, (w ^ bit_wt) * n_dep + (d ^ bit_dep))
            for w in range(n_wt)
            for d in range(n_dep)
            if w % 2 == q
        ]

    inward = [
        (w * n_dep + d, (w ^ 1) * n_dep + d)
        for w in range(n_wt)
        for d in range(n_dep)
        if w % 2 != q
    ]
    over_wt, over_dep = [], []
    bit = 2
    while bit < n_wt:
        over_wt.append((0, (at_wt // bit) % 2, pairs(bit, 0)))
        bit *= 2
    bit = 1
    while bit < n_dep:
        over_dep.append((1, (at_dep // bit) % 2, pairs(0, bit)))
        bit *= 2
    return inward, over_wt + over_dep if q == 0 else over_dep + over_wt


def own_half(gate, upper, half, size):
    first, last = 2 * half * size, 2 * (half + 1) * size
    parts = []
    for whole in (gate, upper):
        part = whole[first : min(last, whole.shape[0])]
        part = jnp.pad(part, ((0, last - first - part.shape[0]), (0, 0)))
        parts.append(part.reshape(2, size, -1))
    return jnp.concatenate(parts, axis=0)


def per_device(n_wt, n_dep, x_saved, out_grad, gate_pre, up_pre, w_gate, w_up, w_down):
    index = lax.axis_index("inp")
    end = (index == 0) | (index == 3)
    k = jnp.stack([index, end]).astype(jnp.int32)
    total = w_down.shape[0]
    size = 16 * -(-total // (16 * GROUPS))
    gate, upper = gate_pre.T, up_pre.T
    wg, wu = w_gate.T, w_up.T

    def rounded(part, got):
        return (part + got.astype(jnp.float32)).astype(jnp.bfloat16)

    own = [own_half(gate, upper, half, size) for half in range(2)]
    swap, middle = [], []
    for step in range(2):
        swap.append(send(own[step], SWAP))
        middle.append(send(own[step], MIDDLE))
    x_whole, grad_whole = (
        lax.all_gather(x_saved, ("wt", "dep"), axis=0, tiled=True),
        lax.all_gather(out_grad, ("wt", "dep"), axis=0, tiled=True),
    )
    part = [sum_group(w_down, grad_whole, a, size, 4) for a in range(GROUPS)]
    down = None
    acc, wgrads = None, (None, None)
    last = GROUPS - 1
    factors = None

    def slots_of(a):
        h = a // 2
        return [own[h], swap[h], swap[2 + h], middle[2 + h], swap[4 + h], middle[h]]

    for step in range(2, 8):
        if step < 4:
            swap[step - 2] = tie(swap[step - 2], part[step - 2])
            middle.append(send(swap[step - 2], MIDDLE))
        if step < 6:
            outward = part[step - 2].astype(jnp.bfloat16)
            payload = jnp.where(end, outward, middle[step - 2])
            swap.append(send(payload, SWAP))
        else:
            swap.append(send(rounded(part[step - 6], middle[step - 2]), TO_ENDS))
        if 4 <= step:
            if step == 7:
                swap[5] = tie(swap[5], down)
            middle.append(send(rounded(part[step - 4], swap[step - 2]), MIDDLE))
        if 6 <= step:
            for a in (2 * step - 12, 2 * step - 11):
                down, *factors = down_group(
                    k, slots_of(a), grad_whole, down, a, size, total, a == last
                )

    def main(a, acc, wgrads, r3, cut=(0, 1)):
        sums = [part[a], swap[2 + a], middle[4 + a], r3]
        args = (k, slots_of(a), sums, x_whole, wg, wu, acc, wgrads)
        acc, *wgrads = main_group(*args, a, cut, size, total)
        return acc, wgrads

    def pieces(value):
        return value.reshape((2, 2) + value.shape[1:])

    middle[6] = tie(middle[6], down)
    cuts = 1 if size % 32 else 2
    rows = size // cuts
    inner = []
    for i in range(cuts):
        cut = slice(i * rows, (i + 1) * rows)
        payload = rounded(part[2][:, cut], middle[6][:, cut])
        if i == 1:
            acc, wgrads = main(0, acc, wgrads, swap[6])
            payload = tie(payload, acc)
        inner.append(send(payload, TO_ENDS))
    if cuts == 1:
        acc, wgrads = main(0, acc, wgrads, swap[6])
    middle[7] = tie(middle[7], acc)
    final = []
    for q in range(2):
        payload = rounded(pieces(part[last])[:, q], pieces(middle[7])[:, q])
        if q == 1:
            acc, wgrads = main(1, acc, wgrads, swap[7])
            payload = tie(payload, acc)
        final.append(send(payload, TO_ENDS))
    for i in range(cuts):
        acc, wgrads = main(2, acc, wgrads, inner[i], (i, cuts))
    sums = [part[last], swap[2 + last], middle[4 + last]]
    gate_grads, up_grads, terms, plans = [], [], [], []
    for q in range(2):
        gate_part, up_part, value, small = token_group(
            k, factors, sums, final[q], wg, wu, acc, q, last, size, total
        )
        gate_grads.append(gate_part)
        up_grads.append(up_part)
        inward, plan = scatter_plan(q, n_wt, n_dep)
        view = (n_wt // 2, n_dep, -1, value.shape[-1])
        got = lax.ppermute(small, ("wt", "dep"), inward)
        terms.append([value.reshape(view), got.reshape(view)])
        plans.append(plan)

    def newest():
        return [t[-1] for t in terms]

    gate_wgrad = weight_group(gate_grads, x_whole, wgrads[0], last, size, newest())
    for stage in range(len(plans[0])):
        terms = [halve(t, *plan[stage]) for t, plan in zip(terms, plans)]
        if stage == 0:
            for t in terms:
                t[-1] = tie(t[-1], gate_wgrad)
            up_wgrad = weight_group(up_grads, x_whole, wgrads[1], last, size, newest())
    shares = [[t[0, 0] for t in of] for of in terms]
    even = lax.axis_index("wt") % 2 == 0
    share = [jnp.where(even, *pair) for pair in zip(*shares)]
    return (total_of(share).astype(jnp.bfloat16), gate_wgrad.T, up_wgrad.T, down)


def solution(mesh):
    placed = (
        P(("wt", "dep"), "inp"),
        P(("wt", "dep"), "inp"),
        P("inp", ("wt", "dep")),
        P("inp", ("wt", "dep")),
        P("inp", ("wt", "dep")),
        P("inp", ("wt", "dep")),
        P(("wt", "dep"), "inp"),
    )
    return jax.shard_map(
        functools.partial(per_device, mesh.shape["wt"], mesh.shape["dep"]),
        mesh=mesh,
        in_specs=placed,
        out_specs=(
            P(("wt", "dep"), "inp"),
            P("inp", ("wt", "dep")),
            P("inp", ("wt", "dep")),
            P(("wt", "dep"), "inp"),
        ),
        check_vma=False,
    )
```
